768 devices in a mesh: replica: 8 (over y), fsdp: 96 (over z, x, core).
Axes of the slice: x: 4, y: 8, z: 12, core: 2. Of those that a mesh axis runs over, the one named last changes fastest.
Arguments:
- grad: bfloat16 [72, 672, 672], P(None, 'fsdp', 'replica')
- owner: int32 [72], replicated, may hold values from 0 to 95, as said below
- row_extent: int32 [72], replicated, may hold values from 336 to 672
- col_extent: int32 [72], replicated, may hold values from 336 to 672
- left_old: float32 [96, 672, 672], P('fsdp', 'replica')
- right_old: float32 [96, 672, 672], P('fsdp', 'replica')
- left_root: float32 [96, 672, 672], P('fsdp')
- right_root: float32 [96, 672, 672], P('fsdp', 'replica'), as said below
Outputs:
- update: bfloat16 [72, 672, 672], P(None, 'fsdp', 'replica')
- left_new: float32 [96, 672, 672], P('fsdp', 'replica')
- right_new: float32 [96, 672, 672], P('fsdp', 'replica')
The draws below stay inside these ranges and needn't reach their ends.
Inputs may be any that keep to these rules, and one draw needn't show every extreme that they name: `owner`: the 72 values are distinct, so that an fsdp index owns at most one block. `right_root`: each of the 96 matrices is symmetric.
All inputs are finite; a program needn't handle non-finite values.
Results may differ from the reference program's by a relative error of at most 0.012.
Values may be sent and summed in bfloat16 or wider, within the bound.
No kernel may reach another device: no remote copies, remote signals or barrier semaphores. Data moves between devices by JAX's collectives and lax.ppermute only.
A program may use at most 32 MiB of HBM per device.

```python
import math
import jax
import jax.numpy as jnp
from jax import lax

BLK = 672
NB = 72
N_FSDP = 96


def symmetric_matrices(jitter, diagonal):
    symmetric = jitter + jnp.swapaxes(jitter, 1, 2)
    identity = jnp.eye(BLK, dtype=jnp.float32)
    return symmetric * (1.0 - identity) + identity * diagonal[:, :, None]


def extent_values(key):
    key_values, key_high, key_low = jax.random.split(key, 3)
    values = jax.random.randint(key_values, (NB,), BLK // 2, BLK + 1)
    high_slot = jax.random.randint(key_high, (), 0, NB)
    low_slot = (high_slot + 1 + jax.random.randint(key_low, (), 0, NB - 1)) % NB
    values = values.at[high_slot].set(BLK)
    values = values.at[low_slot].set(BLK // 2)
    return values.astype(jnp.int32)


def factor_draw(key, spread, lowest, highest):
    key_jitter, key_diagonal = jax.random.split(key)
    jitter = jax.random.normal(key_jitter, (N_FSDP, BLK, BLK), jnp.float32) * spread
    diagonal = jax.random.uniform(key_diagonal, (N_FSDP, BLK), jnp.float32, lowest, highest)
    return symmetric_matrices(jitter, diagonal)


def draw_grad(key, part):
    key = jax.random.fold_in(key, 11)
    key_normal, key_rows, key_cols = jax.random.split(key, 3)
    rising = jnp.exp(math.log(3.0) * jnp.arange(BLK, dtype=jnp.float32) / BLK)
    col_scale = jnp.exp(jax.random.uniform(key_cols, (NB, 1, BLK), jnp.float32, math.log(0.3), math.log(3.0))) * rising
    jitter = jax.random.normal(key_normal, (NB, BLK, BLK), jnp.float32)
    row_scale = jnp.exp(jax.random.uniform(key_rows, (NB, BLK, 1), jnp.float32, math.log(0.3), math.log(3.0)))
    return (jitter * row_scale * col_scale / math.sqrt(BLK)).astype(jnp.bfloat16)


def draw_owner(key, part):
    key = jax.random.fold_in(key, 5)
    key_middle, key_order = jax.random.split(key)
    middle = 1 + jax.random.permutation(key_middle, N_FSDP - 2)
    chosen = jnp.concatenate([jnp.array([0, N_FSDP - 1], dtype=jnp.int32), middle[:NB - 2].astype(jnp.int32)])
    return jax.random.permutation(key_order, chosen).astype(jnp.int32)


def draw_row_extent(key, part):
    key = jax.random.fold_in(key, 7)
    return extent_values(key)


def draw_col_extent(key, part):
    key = jax.random.fold_in(key, 9)
    return extent_values(key)


def draw_left_old(key, part):
    key = jax.random.fold_in(key, 13)
    return factor_draw(key, 0.015, 1.0, 4.0)


def draw_right_old(key, part):
    key = jax.random.fold_in(key, 17)
    return factor_draw(key, 0.015, 1.0, 4.0)


def draw_left_root(key, part):
    key = jax.random.fold_in(key, 19)
    return factor_draw(key, 0.008, 0.8, 1.2)


def draw_right_root(key, part):
    key = jax.random.fold_in(key, 23)
    return factor_draw(key, 0.008, 0.8, 1.2)


def setup_inputs(seed: int = 0) -> dict:
    splits = jax.random.split(jax.random.key(seed), 9)
    return {
        "grad": draw_grad(jax.random.fold_in(splits[8], 71), 0),
        "owner": draw_owner(jax.random.fold_in(splits[8], 71), 0),
        "row_extent": draw_row_extent(jax.random.fold_in(splits[8], 71), 0),
        "col_extent": draw_col_extent(jax.random.fold_in(splits[8], 71), 0),
        "left_old": draw_left_old(jax.random.fold_in(splits[8], 71), 0),
        "right_old": draw_right_old(jax.random.fold_in(splits[8], 71), 0),
        "left_root": draw_left_root(jax.random.fold_in(splits[8], 71), 0),
        "right_root": draw_right_root(jax.random.fold_in(splits[8], 71), 0),
    }


decay_rate = 0.9


def reference(grad, owner, row_extent, col_extent, left_old, right_old, left_root, right_root):
    positions = jnp.arange(BLK, dtype=jnp.int32)

    def one_block(inputs):
        gradient_block, owner_index, row_limit, col_limit = inputs
        live_mask = (positions[:, None] < row_limit) & (positions[None, :] < col_limit)
        masked = jnp.where(live_mask, gradient_block, jnp.zeros_like(gradient_block))
        left_stat = jnp.dot(masked, masked.T, preferred_element_type=jnp.float32)
        right_stat = jnp.dot(masked.T, masked, preferred_element_type=jnp.float32)
        widened = masked.astype(jnp.float32)
        mixed = jnp.dot(left_root[owner_index], widened, precision=lax.Precision.HIGHEST)
        product = jnp.dot(mixed, right_root[owner_index], precision=lax.Precision.HIGHEST)
        product = jnp.where(live_mask, product, jnp.zeros_like(product))
        return left_stat, right_stat, product.astype(jnp.bfloat16)

    left_stat, right_stat, update = lax.map(one_block, (grad, owner, row_extent, col_extent))
    left_new = (decay_rate * left_old).at[owner].add((1.0 - decay_rate) * left_stat)
    right_new = (decay_rate * right_old).at[owner].add((1.0 - decay_rate) * right_stat)
    return update, left_new, right_new
```

```python
import jax
import jax.numpy as jnp
from jax import lax
from jax.sharding import PartitionSpec as P

decay_rate = 0.9


def body(grad, owner, row_extent, col_extent, left_old, right_old, left_root, right_root):
    fsdp_count = lax.axis_size("fsdp")
    fsdp_index = lax.axis_index("fsdp")
    replica_index = lax.axis_index("replica")
    row_share = grad.shape[1]
    col_share = grad.shape[2]
    block_order = row_share * fsdp_count
    row_index = fsdp_index * row_share + jnp.arange(row_share, dtype=jnp.int32)
    col_index = replica_index * col_share + jnp.arange(col_share, dtype=jnp.int32)
    live_mask = (row_index[None, :, None] < row_extent[:, None, None]) & (
        col_index[None, None, :] < col_extent[:, None, None]
    )
    masked = jnp.where(live_mask, grad, jnp.zeros_like(grad))
    owners = jnp.arange(fsdp_count, dtype=jnp.int32)
    select = (owner[None, :] == owners[:, None]).astype(jnp.bfloat16)
    outgoing = jnp.einsum("ob,bic->oci", select, masked, preferred_element_type=jnp.float32).astype(
        jnp.bfloat16
    )
    columns = lax.all_to_all(outgoing, "fsdp", split_axis=0, concat_axis=2, tiled=True)[0]
    owned_mask = owner == fsdp_index
    owned_rows = jnp.sum(jnp.where(owned_mask, row_extent, 0))
    owned_cols = jnp.sum(jnp.where(owned_mask, col_extent, 0))
    rows_start = replica_index * col_share
    root_rows = right_root[0]
    incoming = lax.all_gather(columns, "replica", axis=0, tiled=True)
    right_part = jnp.einsum("cm,km->ck", columns, incoming, preferred_element_type=jnp.float32)
    right_rows = right_part
    weighted = jnp.dot(root_rows, incoming.astype(jnp.float32), precision=lax.Precision.HIGHEST)
    row_slice = lax.dynamic_slice_in_dim(incoming, rows_start, col_share, 1)
    left_rows = jnp.einsum("ci,cj->ij", row_slice, incoming, preferred_element_type=jnp.float32)
    transposed = jnp.einsum("jm,im->ji", weighted, left_root[0], precision=lax.Precision.HIGHEST)
    block_rows = jnp.arange(block_order, dtype=jnp.int32)
    keep_mask = (block_rows[None, :] < owned_rows) & (col_index[:, None] < owned_cols)
    result = jnp.where(keep_mask, transposed, jnp.zeros_like(transposed)).astype(jnp.bfloat16)
    returned = lax.all_to_all(
        result.reshape(col_share, fsdp_count, row_share),
        "fsdp",
        split_axis=1,
        concat_axis=1,
        tiled=True,
    )
    update = jnp.einsum("ob,joi->bij", select, returned, preferred_element_type=jnp.float32).astype(
        jnp.bfloat16
    )
    left_new = decay_rate * left_old + ((1.0 - decay_rate) * left_rows)[None]
    right_new = decay_rate * right_old + ((1.0 - decay_rate) * right_rows)[None]
    return (update, left_new, right_new)


def solution(mesh):
    placed = (
        P(None, "fsdp", "replica"),
        P(),
        P(),
        P(),
        P("fsdp", "replica", None),
        P("fsdp", "replica", None),
        P("fsdp", None, None),
        P("fsdp", "replica", None),
    )
    return jax.shard_map(
        body,
        mesh=mesh,
        in_specs=placed,
        out_specs=(
            P(None, "fsdp", "replica"),
            P("fsdp", "replica", None),
            P("fsdp", "replica", None),
        ),
        check_vma=False,
    )
```

```python
import functools

import jax
import jax.numpy as jnp
from jax import lax
from jax.experimental import pallas as pl
from jax.experimental.pallas import tpu as pltpu
from jax.sharding import PartitionSpec as P

decay_rate = 0.9
lane_count = 128
slot_rows = 8
f32 = jnp.float32
bf16 = jnp.bfloat16
vmem = pl.BlockSpec(memory_space=pltpu.VMEM)
smem = pl.BlockSpec(memory_space=pltpu.SMEM)


def call(kernel, out_shape, in_specs, name, flops, scratch=()):
    return pl.pallas_call(
        kernel,
        out_shape=out_shape,
        in_specs=in_specs,
        out_specs=jax.tree.map(lambda _: vmem, out_shape),
        scratch_shapes=list(scratch),
        compiler_params=pltpu.CompilerParams(vmem_limit_bytes=48 * 2**20),
        cost_estimate=pl.CostEstimate(flops=flops, bytes_accessed=2**20, transcendentals=0),
        name=name,
    )


def iota(shape, dim):
    return lax.broadcasted_iota(jnp.int32, shape, dim)


def rounded_up(value, step):
    return -(-value // step) * step


def one_hot(condition):
    return condition.astype(f32).astype(bf16)


def pack_kernel(owner_ref, grad_ref, wire_ref, slots):
    row_share, block_count, col_share = grad_ref.shape
    fsdp_count = wire_ref.shape[0] // slot_rows
    slots[...] = jnp.zeros_like(slots)
    pick = one_hot(iota((fsdp_count, block_count), 0) == owner_ref[...])
    for i in range(row_share):
        slots[pl.ds(i, fsdp_count, stride=slot_rows), :col_share] = jnp.dot(
            pick, grad_ref[i], preferred_element_type=f32
        )
    wire_ref[...] = slots[...].astype(bf16)


def unpack_kernel(owner_ref, wire_ref, update_ref, slots):
    row_share, block_count, col_share = update_ref.shape
    fsdp_count = wire_ref.shape[0] // slot_rows
    slots[...] = wire_ref[...].astype(f32)
    pick = one_hot(iota((fsdp_count, block_count), 0) == owner_ref[...])
    for i in range(row_share):
        rows = slots[pl.ds(i, fsdp_count, stride=slot_rows), :].astype(bf16)
        picked = lax.dot_general(pick, rows, (((0,), (0,)), ((), ())), preferred_element_type=f32)
        update_ref[i] = picked[:, :col_share].astype(bf16)


def prepare_kernel(row_share, left_ref, right_ref, left_high_ref, left_low_ref, right_ref_out):
    wire_rows, block_order = left_high_ref.shape
    row = iota((wire_rows, block_order), 0)
    place = (row // slot_rows) * row_share + row % slot_rows
    spread = one_hot((place == iota((wire_rows, block_order), 1)) & (row % slot_rows < row_share))
    left = left_ref[...]
    left_high = left.astype(bf16)
    left_low = (left - left_high.astype(f32)).astype(bf16)
    left_high_ref[...] = jnp.dot(spread, left_high, preferred_element_type=f32).astype(bf16)
    left_low_ref[...] = jnp.dot(spread, left_low, preferred_element_type=f32).astype(bf16)
    replica_count, piece_rows, col_share = right_ref_out.shape
    right = right_ref[...]
    right_high = right.astype(bf16).astype(f32)
    right_low = right - right_high
    filler = jnp.zeros((piece_rows // 2 - col_share, col_share), f32)
    for s in range(replica_count):
        part = slice(s * col_share, (s + 1) * col_share)
        right_ref_out[s] = jnp.concatenate(
            [right_high[:, part], filler, right_low[:, part], filler], axis=0
        ).astype(bf16)


def turn_kernel(row_share, extent_ref, wire_ref, columns_ref, slots, rows):
    col_share, block_order = columns_ref.shape
    fsdp_count = wire_ref.shape[0] // slot_rows
    slots[...] = wire_ref[...].astype(f32)
    for i in range(row_share):
        rows[pl.ds(i, fsdp_count, stride=row_share), :] = slots[
            pl.ds(i, fsdp_count, stride=slot_rows), :
        ]
    turned = rows[...].T[:col_share]
    shape = (col_share, block_order)
    keep = (iota(shape, 0) + extent_ref[2] < extent_ref[1]) & (iota(shape, 1) < extent_ref[0])
    columns_ref[...] = jnp.where(keep, turned, 0.0).astype(bf16)


def update_kernel(row_share, extent_ref, block_ref, right_ref, left_high_ref, left_low_ref, wire_ref):
    replica_count, col_share, block_order = block_ref.shape
    half = right_ref.shape[1] // 2
    total = jnp.dot(right_ref[0], block_ref[0], preferred_element_type=f32)
    for s in range(1, replica_count):
        total += jnp.dot(right_ref[s], block_ref[s], preferred_element_type=f32)
    product = total[:half] + total[half:]
    product = jnp.concatenate(
        [product, jnp.zeros((lane_count - half, block_order), f32)], axis=0
    )
    high = product.astype(bf16)
    low = (product - high.astype(f32)).astype(bf16)
    last = (((1,), (1,)), ((), ()))
    first = lax.dot_general(
        left_high_ref[...], jnp.concatenate([high, low], axis=0), last, preferred_element_type=f32
    )
    second = lax.dot_general(left_low_ref[...], high, last, preferred_element_type=f32)
    result = first[:, :lane_count] + first[:, lane_count:] + second
    row = iota(wire_ref.shape, 0)
    lane = iota(wire_ref.shape, 1)
    place = (row // slot_rows) * row_share + row % slot_rows
    keep = (
        (place < extent_ref[0])
        & (row % slot_rows < row_share)
        & (lane + extent_ref[2] < extent_ref[1])
        & (lane < col_share)
    )
    wire_ref[...] = jnp.where(keep, result, 0.0).astype(bf16)


def body(grad, owner, row_extent, col_extent, left_old, right_old, left_root, right_root):
    fsdp_count = lax.axis_size("fsdp")
    fsdp_index = lax.axis_index("fsdp")
    replica_count = lax.axis_size("replica")
    replica_index = lax.axis_index("replica")
    block_count, row_share, col_share = grad.shape
    block_order = row_share * fsdp_count
    wire_shape = (fsdp_count * slot_rows, lane_count)
    wire = jax.ShapeDtypeStruct(wire_shape, bf16)
    slots = pltpu.VMEM(wire_shape, f32)
    owner_row = owner[None, :]

    outgoing = call(pack_kernel, wire, [vmem, vmem], "pack", 2**20, [slots])(
        owner_row, grad.transpose(1, 0, 2)
    )
    received = lax.all_to_all(outgoing, "fsdp", split_axis=0, concat_axis=0, tiled=True)

    owned_mask = owner == fsdp_index
    rows_start = replica_index * col_share
    extents = jnp.stack(
        [
            jnp.sum(jnp.where(owned_mask, row_extent, 0)),
            jnp.sum(jnp.where(owned_mask, col_extent, 0)),
            rows_start,
        ]
    ).astype(jnp.int32)
    spread_shape = jax.ShapeDtypeStruct((wire_shape[0], block_order), bf16)
    half = rounded_up(col_share, 16)
    left_high, left_low, right_pieces = call(
        functools.partial(prepare_kernel, row_share),
        [
            spread_shape,
            spread_shape,
            jax.ShapeDtypeStruct((replica_count, 2 * half, col_share), bf16),
        ],
        [vmem, vmem],
        "prepare",
        2**31,
    )(left_root[0], right_root[0])

    columns = call(
        functools.partial(turn_kernel, row_share),
        jax.ShapeDtypeStruct((col_share, block_order), bf16),
        [smem, vmem],
        "turn",
        2**20,
        [slots, pltpu.VMEM((block_order, lane_count), f32)],
    )(extents, received)
    block = lax.all_gather(columns, "replica", axis=0)
    result = call(
        functools.partial(update_kernel, row_share),
        wire,
        [smem, vmem, vmem, vmem, vmem],
        "update",
        2**30,
    )(extents, block, right_pieces, left_high, left_low)
    returned = lax.all_to_all(result, "fsdp", split_axis=0, concat_axis=0, tiled=True)

    transposed = block.reshape(block_order, block_order)
    row_slice = lax.dynamic_slice_in_dim(transposed, rows_start, col_share, 1)
    left_rows = jnp.einsum("ci,cj->ij", row_slice, transposed, preferred_element_type=f32)
    right_rows = jnp.einsum("cm,km->ck", columns, transposed, preferred_element_type=f32)
    left_new = decay_rate * left_old + ((1.0 - decay_rate) * left_rows)[None]
    right_new = decay_rate * right_old + ((1.0 - decay_rate) * right_rows)[None]

    update = call(
        unpack_kernel,
        jax.ShapeDtypeStruct((row_share, block_count, col_share), bf16),
        [vmem, vmem],
        "unpack",
        2**20,
        [slots],
    )(owner_row, returned)
    return (update.transpose(1, 0, 2), left_new, right_new)


def solution(mesh):
    placed = (
        P(None, "fsdp", "replica"),
        P(),
        P(),
        P(),
        P("fsdp", "replica", None),
        P("fsdp", "replica", None),
        P("fsdp", None, None),
        P("fsdp", "replica", None),
    )
    return jax.shard_map(
        body,
        mesh=mesh,
        in_specs=placed,
        out_specs=(
            P(None, "fsdp", "replica"),
            P("fsdp", "replica", None),
            P("fsdp", "replica", None),
        ),
        check_vma=False,
    )
```

```python
import functools

import jax
import jax.numpy as jnp
from jax import lax
from jax.experimental import pallas as pl
from jax.experimental.pallas import tpu as pltpu
from jax.sharding import PartitionSpec as P

decay_rate = 0.9
lane_count = 128
wire_halves = 2
f32 = jnp.float32
bf16 = jnp.bfloat16
vmem = pl.BlockSpec(memory_space=pltpu.VMEM)
hbm = pl.BlockSpec(memory_space=pltpu.HBM)


def call(kernel, out_shape, in_specs, name, flops, scratch=(), out_specs=None):
    return pl.pallas_call(
        kernel,
        out_shape=out_shape,
        in_specs=in_specs,
        out_specs=out_specs or jax.tree.map(lambda _: vmem, out_shape),
        scratch_shapes=list(scratch),
        compiler_params=pltpu.CompilerParams(vmem_limit_bytes=20 * 2**20),
        cost_estimate=pl.CostEstimate(flops=flops, bytes_accessed=2**20, transcendentals=0),
        name=name,
    )


def iota(shape, dim):
    return lax.broadcasted_iota(jnp.int32, shape, dim)


def rounded_up(value, step):
    return -(-value // step) * step


def one_hot(condition):
    return condition.astype(f32).astype(bf16)


def pitch_of(col_share):
    return rounded_up(col_share, 32)


def per_half_of(row_share):
    return -(-row_share // wire_halves)


def wire_lanes(row_share, col_share):
    return rounded_up(per_half_of(row_share) * pitch_of(col_share), lane_count)


def joined(pieces, lanes):
    rows = pieces[0].shape[0]
    width = sum(p.shape[1] for p in pieces)
    if width < lanes:
        pieces = [*pieces, jnp.zeros((rows, lanes - width), pieces[0].dtype)]
    return jnp.concatenate(pieces, axis=1)


def tiles(lanes):
    return [slice(t * lane_count, (t + 1) * lane_count) for t in range(lanes // lane_count)]


def put_half(slots, h, value):
    for t, part in enumerate(tiles(value.shape[1])):
        slots[t, pl.ds(h, value.shape[0], stride=wire_halves), :] = value[:, part]


def get_half(slots, h):
    count = slots.shape[1] // wire_halves
    return jnp.concatenate(
        [slots[t, pl.ds(h, count, stride=wire_halves), :] for t in range(slots.shape[0])], axis=1
    )


def to_wire(slots, wire_ref):
    owners, halves, lanes = wire_ref.shape
    for t, part in enumerate(tiles(lanes)):
        wire_ref[:, :, part] = slots[t].astype(bf16).reshape(owners, halves, lane_count)


def from_wire(slots, wire_ref):
    owners, halves, lanes = wire_ref.shape
    for t, part in enumerate(tiles(lanes)):
        slots[t] = wire_ref[:, :, part].reshape(owners * halves, lane_count).astype(f32)


def pack_kernel(owner_hbm, grad_hbm, wire_ref, owner_ref, grad_ref, slots, sems):
    copies = [
        pltpu.make_async_copy(owner_hbm, owner_ref, sems.at[0]),
        pltpu.make_async_copy(grad_hbm, grad_ref, sems.at[1]),
    ]
    for copy in copies:
        copy.start()
    for copy in copies:
        copy.wait()
    row_share, block_count, col_share = grad_ref.shape
    fsdp_count, _, lanes = wire_ref.shape
    per_half = per_half_of(row_share)
    gap = jnp.zeros((block_count, pitch_of(col_share) - col_share), bf16)
    pick = one_hot(iota((fsdp_count, block_count), 0) == owner_ref[...])
    for h in range(wire_halves):
        pieces = []
        for i in range(h * per_half, min(row_share, (h + 1) * per_half)):
            pieces += [grad_ref[i], gap]
        put_half(
            slots, h, jnp.dot(pick, joined(pieces, lanes), preferred_element_type=f32)
        )
    to_wire(slots, wire_ref)


def unpack_kernel(owner_ref, wire_ref, update_ref, slots):
    row_share, block_count, col_share = update_ref.shape
    fsdp_count = wire_ref.shape[0]
    per_half = per_half_of(row_share)
    pitch = pitch_of(col_share)
    from_wire(slots, wire_ref)
    pick = one_hot(iota((fsdp_count, block_count), 0) == owner_ref[...])
    for h in range(wire_halves):
        rows = get_half(slots, h).astype(bf16)
        picked = lax.dot_general(pick, rows, (((0,), (0,)), ((), ())), preferred_element_type=f32)
        for i in range(h * per_half, min(row_share, (h + 1) * per_half)):
            start = (i - h * per_half) * pitch
            update_ref[i] = picked[:, start : start + col_share].astype(bf16)


def order_matrix(row_share, fsdp_count, forward):
    parts = []
    for i in range(row_share):
        shape = (fsdp_count, row_share * fsdp_count)
        if not forward:
            shape = shape[::-1]
        place, index = (0, 1) if forward else (1, 0)
        parts.append(iota(shape, place) * row_share + i == iota(shape, index))
    parts = [one_hot(p) for p in parts]
    return jnp.concatenate(parts, axis=0 if forward else 1)


def prepare_kernel(row_share, left_ref, right_ref, split_hbm, pieces_ref, split_ref, sem):
    block_order = left_ref.shape[0]
    fsdp_count = block_order // row_share
    rows = order_matrix(row_share, fsdp_count, True)
    cols = order_matrix(row_share, fsdp_count, False)
    left = left_ref[...]
    left_high = left.astype(bf16)
    left_low = (left - left_high.astype(f32)).astype(bf16)
    for n, part in enumerate((left_high, left_low)):
        half_done = jnp.dot(rows, part, preferred_element_type=f32).astype(bf16)
        split_ref[n] = jnp.dot(half_done, cols, preferred_element_type=f32).astype(bf16)
    copy = pltpu.make_async_copy(split_ref, split_hbm, sem.at[0])
    copy.start()
    replica_count, piece_rows, col_share = pieces_ref.shape
    right = right_ref[...]
    right_high = right.astype(bf16).astype(f32)
    right_low = right - right_high
    filler = jnp.zeros((piece_rows // 2 - col_share, col_share), f32)
    for s in range(replica_count):
        part = slice(s * col_share, (s + 1) * col_share)
        pieces_ref[s] = jnp.concatenate(
            [right_high[:, part], filler, right_low[:, part], filler], axis=0
        ).astype(bf16)
    copy.wait()


def owned_extent(owner_ref, extent_ref):
    mine = owner_ref[...] == lax.axis_index("fsdp")
    values = jnp.where(mine, extent_ref[...], 0).astype(f32)
    return jnp.sum(values, axis=1, keepdims=True).astype(jnp.int32)


def turn_kernel(row_share, owner_ref, rows_ref, cols_ref, wire_ref, columns_ref, slots):
    col_share, block_order = columns_ref.shape
    fsdp_count = wire_ref.shape[0]
    per_half = per_half_of(row_share)
    pitch = pitch_of(col_share)
    live_rows = owned_extent(owner_ref, rows_ref)
    live_cols = owned_extent(owner_ref, cols_ref) - lax.axis_index("replica") * col_share
    from_wire(slots, wire_ref)
    shape = (col_share, fsdp_count)
    col_live = iota(shape, 0) < live_cols
    pieces = []
    for h in range(wire_halves):
        turned = get_half(slots, h).T
        for i in range(h * per_half, min(row_share, (h + 1) * per_half)):
            start = (i - h * per_half) * pitch
            keep = col_live & (iota(shape, 1) * row_share + i < live_rows)
            pieces.append(jnp.where(keep, turned[start : start + col_share], 0.0))
    columns_ref[...] = jnp.concatenate(pieces, axis=1).astype(bf16)


def update_kernel(
    row_share, owner_ref, rows_ref, cols_ref, block_ref, right_ref, left_hbm, wire_ref, slots,
    left_ref, sem,
):
    copy = pltpu.make_async_copy(left_hbm, left_ref, sem.at[0])
    copy.start()
    replica_count, col_share, block_order = block_ref.shape
    fsdp_count = block_order // row_share
    per_half = per_half_of(row_share)
    pitch = pitch_of(col_share)
    half = right_ref.shape[1] // 2
    live_rows = owned_extent(owner_ref, rows_ref)
    live_cols = owned_extent(owner_ref, cols_ref) - lax.axis_index("replica") * col_share
    total = jnp.dot(right_ref[0], block_ref[0], preferred_element_type=f32)
    for s in range(1, replica_count):
        total += jnp.dot(right_ref[s], block_ref[s], preferred_element_type=f32)
    product = total[:half] + total[half:]
    product = jnp.concatenate(
        [product, jnp.zeros((lane_count - half, block_order), f32)], axis=0
    )
    high = product.astype(bf16)
    low = (product - high.astype(f32)).astype(bf16)
    last = (((1,), (1,)), ((), ()))
    copy.wait()
    first = lax.dot_general(
        left_ref[0], jnp.concatenate([high, low], axis=0), last, preferred_element_type=f32
    )
    second = lax.dot_general(left_ref[1], high, last, preferred_element_type=f32)
    result = first[:, :lane_count] + first[:, lane_count:] + second
    shape = (fsdp_count, lane_count)
    lane = iota(shape, 1)
    col_live = (lane < live_cols) & (lane < col_share)
    for h in range(wire_halves):
        pieces = []
        for i in range(h * per_half, min(row_share, (h + 1) * per_half)):
            keep = col_live & (iota(shape, 0) * row_share + i < live_rows)
            piece = jnp.where(keep, result[i * fsdp_count : (i + 1) * fsdp_count], 0.0)
            pieces.append(piece[:, :pitch])
        put_half(slots, h, joined(pieces, wire_ref.shape[2]))
    to_wire(slots, wire_ref)


def stats_kernel(row_share, block_ref, columns_ref, after_ref, left_ref, right_ref):
    replica_count, col_share, block_order = block_ref.shape
    fsdp_count = block_order // row_share
    order = order_matrix(row_share, fsdp_count, True)
    rows_start = lax.axis_index("replica") * col_share
    mine = one_hot(
        (iota((block_order, col_share), 0) == iota((block_order, col_share), 1) + rows_start)
    )
    columns = columns_ref[...]
    left = jnp.zeros(left_ref.shape, f32)
    for s in range(replica_count):
        part = jnp.dot(block_ref[s], order, preferred_element_type=f32).astype(bf16)
        picked = jnp.dot(part, mine, preferred_element_type=f32).astype(bf16)
        left += lax.dot_general(
            picked, part, (((0,), (0,)), ((), ())), preferred_element_type=f32
        )
        right_ref[:, s * col_share : (s + 1) * col_share] = lax.dot_general(
            columns, block_ref[s], (((1,), (1,)), ((), ())), preferred_element_type=f32
        )
    left_ref[...] = left


def body(grad, owner, row_extent, col_extent, left_old, right_old, left_root, right_root):
    fsdp_count = lax.axis_size("fsdp")
    replica_count = lax.axis_size("replica")
    block_count, row_share, col_share = grad.shape
    block_order = row_share * fsdp_count
    lanes = wire_lanes(row_share, col_share)
    wire = jax.ShapeDtypeStruct((fsdp_count, wire_halves, lanes), bf16)
    slots = pltpu.VMEM((lanes // lane_count, fsdp_count * wire_halves, lane_count), f32)
    owner_row, live_rows, live_cols = owner[None, :], row_extent[None, :], col_extent[None, :]
    turned_grad = grad.transpose(1, 0, 2)

    def exchange(sent):
        return lax.all_to_all(sent, "fsdp", split_axis=0, concat_axis=0, tiled=True)

    received = exchange(
        call(
            pack_kernel,
            wire,
            [hbm, hbm],
            "pack",
            2**20,
            [
                pltpu.VMEM(owner_row.shape, jnp.int32),
                pltpu.VMEM(turned_grad.shape, bf16),
                slots,
                pltpu.SemaphoreType.DMA((2,)),
            ],
        )(pltpu.with_memory_space_constraint(owner_row, pltpu.HBM),
          pltpu.with_memory_space_constraint(turned_grad, pltpu.HBM))
    )

    root_shape = jax.ShapeDtypeStruct((2, block_order, block_order), bf16)
    half = rounded_up(col_share, 16)
    left_split, right_pieces = call(
        functools.partial(prepare_kernel, row_share),
        [
            root_shape,
            jax.ShapeDtypeStruct((replica_count, 2 * half, col_share), bf16),
        ],
        [vmem, vmem],
        "prepare",
        2**31,
        [pltpu.VMEM(root_shape.shape, bf16), pltpu.SemaphoreType.DMA((1,))],
        [hbm, vmem],
    )(left_root[0], right_root[0])

    columns = call(
        functools.partial(turn_kernel, row_share),
        jax.ShapeDtypeStruct((col_share, block_order), bf16),
        [vmem] * 4,
        "turn",
        2**20,
        [slots],
    )(owner_row, live_rows, live_cols, received)
    block = lax.all_gather(columns, "replica", axis=0)
    result = call(
        functools.partial(update_kernel, row_share),
        wire,
        [vmem] * 5 + [hbm],
        "update",
        2**30,
        [slots, pltpu.VMEM(root_shape.shape, bf16), pltpu.SemaphoreType.DMA((1,))],
    )(
        owner_row,
        live_rows,
        live_cols,
        block,
        right_pieces,
        pltpu.with_memory_space_constraint(left_split, pltpu.HBM),
    )
    returned = exchange(result)

    stat = jax.ShapeDtypeStruct((col_share, block_order), f32)
    left_rows, right_rows = call(
        functools.partial(stats_kernel, row_share),
        [stat, stat],
        [vmem, vmem, hbm],
        "stats",
        2**29,
    )(block, columns, result)
    left_new = decay_rate * left_old + ((1.0 - decay_rate) * left_rows)[None]
    right_new = decay_rate * right_old + ((1.0 - decay_rate) * right_rows)[None]

    update = call(
        unpack_kernel,
        jax.ShapeDtypeStruct((row_share, block_count, col_share), bf16),
        [vmem, vmem],
        "unpack",
        2**20,
        [slots],
    )(owner_row, returned)
    return (update.transpose(1, 0, 2), left_new, right_new)


def solution(mesh):
    placed = (
        P(None, "fsdp", "replica"),
        P(),
        P(),
        P(),
        P("fsdp", "replica", None),
        P("fsdp", "replica", None),
        P("fsdp", None, None),
        P("fsdp", "replica", None),
    )
    return jax.shard_map(
        body,
        mesh=mesh,
        in_specs=placed,
        out_specs=(
            P(None, "fsdp", "replica"),
            P("fsdp", "replica", None),
            P("fsdp", "replica", None),
        ),
        check_vma=False,
    )
```

```python
import functools

import jax
import jax.numpy as jnp
from jax import lax
from jax.experimental import pallas as pl
from jax.experimental.pallas import tpu as pltpu
from jax.sharding import PartitionSpec as P

decay_rate = 0.9
lane_count = 128
wire_halves = 2
f32 = jnp.float32
bf16 = jnp.bfloat16
vmem = pl.BlockSpec(memory_space=pltpu.VMEM)
hbm = pl.BlockSpec(memory_space=pltpu.HBM)


def call(kernel, out_shape, in_specs, name, flops, scratch=(), out_specs=None):
    return pl.pallas_call(
        kernel,
        out_shape=out_shape,
        in_specs=in_specs,
        out_specs=out_specs or jax.tree.map(lambda _: vmem, out_shape),
        scratch_shapes=list(scratch),
        compiler_params=pltpu.CompilerParams(vmem_limit_bytes=20 * 2**20),
        cost_estimate=pl.CostEstimate(flops=flops, bytes_accessed=2**20, transcendentals=0),
        name=name,
    )


def iota(shape, dim):
    return lax.broadcasted_iota(jnp.int32, shape, dim)


def rounded_up(value, step):
    return -(-value // step) * step


def one_hot(condition):
    return condition.astype(f32).astype(bf16)


def pitch_of(col_share):
    return rounded_up(col_share, 32)


def per_half_of(row_share):
    return -(-row_share // wire_halves)


def wire_lanes(row_share, col_share):
    return rounded_up(per_half_of(row_share) * pitch_of(col_share), lane_count)


def joined(pieces, lanes):
    rows = pieces[0].shape[0]
    width = sum(p.shape[1] for p in pieces)
    if width < lanes:
        pieces = [*pieces, jnp.zeros((rows, lanes - width), pieces[0].dtype)]
    return jnp.concatenate(pieces, axis=1)


def tiles(lanes):
    return [slice(t * lane_count, (t + 1) * lane_count) for t in range(lanes // lane_count)]


def put_half(slots, h, value):
    for t, part in enumerate(tiles(value.shape[1])):
        slots[t, pl.ds(h, value.shape[0], stride=wire_halves), :] = value[:, part]


def get_half(slots, h):
    count = slots.shape[1] // wire_halves
    return jnp.concatenate(
        [slots[t, pl.ds(h, count, stride=wire_halves), :] for t in range(slots.shape[0])], axis=1
    )


def to_wire(slots, wire_ref):
    owners, halves, lanes = wire_ref.shape
    for t, part in enumerate(tiles(lanes)):
        wire_ref[:, :, part] = slots[t].astype(bf16).reshape(owners, halves, lane_count)


def from_wire(slots, wire_ref):
    owners, halves, lanes = wire_ref.shape
    for t, part in enumerate(tiles(lanes)):
        slots[t] = wire_ref[:, :, part].reshape(owners * halves, lane_count).astype(f32)


def pack_kernel(owner_hbm, grad_hbm, wire_ref, owner_ref, grad_ref, slots, sems):
    copies = [
        pltpu.make_async_copy(owner_hbm, owner_ref, sems.at[0]),
        pltpu.make_async_copy(grad_hbm, grad_ref, sems.at[1]),
    ]
    for copy in copies:
        copy.start()
    for copy in copies:
        copy.wait()
    row_share, block_count, col_share = grad_ref.shape
    fsdp_count, _, lanes = wire_ref.shape
    per_half = per_half_of(row_share)
    gap = jnp.zeros((block_count, pitch_of(col_share) - col_share), bf16)
    pick = one_hot(iota((fsdp_count, block_count), 0) == owner_ref[...])
    for h in range(wire_halves):
        pieces = []
        for i in range(h * per_half, min(row_share, (h + 1) * per_half)):
            pieces += [grad_ref[i], gap]
        put_half(
            slots, h, jnp.dot(pick, joined(pieces, lanes), preferred_element_type=f32)
        )
    to_wire(slots, wire_ref)


def unpack_kernel(owner_ref, wire_ref, update_ref, slots):
    row_share, block_count, col_share = update_ref.shape
    fsdp_count = wire_ref.shape[0]
    per_half = per_half_of(row_share)
    pitch = pitch_of(col_share)
    from_wire(slots, wire_ref)
    pick = one_hot(iota((fsdp_count, block_count), 0) == owner_ref[...])
    for h in range(wire_halves):
        rows = get_half(slots, h).astype(bf16)
        picked = lax.dot_general(pick, rows, (((0,), (0,)), ((), ())), preferred_element_type=f32)
        for i in range(h * per_half, min(row_share, (h + 1) * per_half)):
            start = (i - h * per_half) * pitch
            update_ref[i] = picked[:, start : start + col_share].astype(bf16)


def order_matrix(row_share, fsdp_count, forward):
    parts = []
    for i in range(row_share):
        shape = (fsdp_count, row_share * fsdp_count)
        if not forward:
            shape = shape[::-1]
        place, index = (0, 1) if forward else (1, 0)
        parts.append(iota(shape, place) * row_share + i == iota(shape, index))
    parts = [one_hot(p) for p in parts]
    return jnp.concatenate(parts, axis=0 if forward else 1)


def prepare_kernel(
    row_share, left_ref, right_ref, left_high_ref, left_low_hbm, pieces_ref, left_low_ref, sem
):
    block_order = left_ref.shape[0]
    fsdp_count = block_order // row_share
    rows = order_matrix(row_share, fsdp_count, True)
    cols = order_matrix(row_share, fsdp_count, False)
    left = left_ref[...]
    left_high = left.astype(bf16)
    left_low = (left - left_high.astype(f32)).astype(bf16)
    for part, ref in ((left_low, left_low_ref), (left_high, left_high_ref)):
        half_done = jnp.dot(rows, part, preferred_element_type=f32).astype(bf16)
        ref[...] = jnp.dot(half_done, cols, preferred_element_type=f32).astype(bf16)
    copy = pltpu.make_async_copy(left_low_ref, left_low_hbm, sem.at[0])
    copy.start()
    replica_count, piece_rows, col_share = pieces_ref.shape
    right = right_ref[...]
    right_high = right.astype(bf16).astype(f32)
    right_low = right - right_high
    filler = jnp.zeros((piece_rows // 2 - col_share, col_share), f32)
    for s in range(replica_count):
        part = slice(s * col_share, (s + 1) * col_share)
        pieces_ref[s] = jnp.concatenate(
            [right_high[:, part], filler, right_low[:, part], filler], axis=0
        ).astype(bf16)
    copy.wait()


def owned_extent(owner_ref, extent_ref):
    mine = owner_ref[...] == lax.axis_index("fsdp")
    values = jnp.where(mine, extent_ref[...], 0).astype(f32)
    return jnp.sum(values, axis=1, keepdims=True).astype(jnp.int32)


def turn_kernel(row_share, owner_ref, rows_ref, cols_ref, wire_ref, columns_ref, slots):
    col_share, block_order = columns_ref.shape
    fsdp_count = wire_ref.shape[0]
    per_half = per_half_of(row_share)
    pitch = pitch_of(col_share)
    live_rows = owned_extent(owner_ref, rows_ref)
    live_cols = owned_extent(owner_ref, cols_ref) - lax.axis_index("replica") * col_share
    from_wire(slots, wire_ref)
    shape = (col_share, fsdp_count)
    col_live = iota(shape, 0) < live_cols
    pieces = []
    for h in range(wire_halves):
        turned = get_half(slots, h).T
        for i in range(h * per_half, min(row_share, (h + 1) * per_half)):
            start = (i - h * per_half) * pitch
            keep = col_live & (iota(shape, 1) * row_share + i < live_rows)
            pieces.append(jnp.where(keep, turned[start : start + col_share], 0.0))
    columns_ref[...] = jnp.concatenate(pieces, axis=1).astype(bf16)


def update_kernel(
    row_share, owner_ref, rows_ref, cols_ref, block_ref, right_ref, left_high_ref, left_low_hbm,
    wire_ref, slots, left_low_ref, sem,
):
    copy = pltpu.make_async_copy(left_low_hbm, left_low_ref, sem.at[0])
    copy.start()
    replica_count, col_share, block_order = block_ref.shape
    fsdp_count = block_order // row_share
    per_half = per_half_of(row_share)
    pitch = pitch_of(col_share)
    half = right_ref.shape[1] // 2
    live_rows = owned_extent(owner_ref, rows_ref)
    live_cols = owned_extent(owner_ref, cols_ref) - lax.axis_index("replica") * col_share
    total = jnp.dot(right_ref[0], block_ref[0], preferred_element_type=f32)
    for s in range(1, replica_count):
        total += jnp.dot(right_ref[s], block_ref[s], preferred_element_type=f32)
    product = total[:half] + total[half:]
    product = jnp.concatenate(
        [product, jnp.zeros((lane_count - half, block_order), f32)], axis=0
    )
    high = product.astype(bf16)
    low = (product - high.astype(f32)).astype(bf16)
    last = (((1,), (1,)), ((), ()))
    first = lax.dot_general(
        left_high_ref[...], jnp.concatenate([high, low], axis=0), last, preferred_element_type=f32
    )
    copy.wait()
    second = lax.dot_general(left_low_ref[...], high, last, preferred_element_type=f32)
    result = first[:, :lane_count] + first[:, lane_count:] + second
    shape = (fsdp_count, lane_count)
    lane = iota(shape, 1)
    col_live = (lane < live_cols) & (lane < col_share)
    for h in range(wire_halves):
        pieces = []
        for i in range(h * per_half, min(row_share, (h + 1) * per_half)):
            keep = col_live & (iota(shape, 0) * row_share + i < live_rows)
            piece = jnp.where(keep, result[i * fsdp_count : (i + 1) * fsdp_count], 0.0)
            pieces.append(piece[:, :pitch])
        put_half(slots, h, joined(pieces, wire_ref.shape[2]))
    to_wire(slots, wire_ref)


def stats_kernel(row_share, block_ref, columns_ref, after_ref, left_ref, right_ref):
    replica_count, col_share, block_order = block_ref.shape
    fsdp_count = block_order // row_share
    order = order_matrix(row_share, fsdp_count, True)
    rows_start = lax.axis_index("replica") * col_share
    mine = one_hot(
        (iota((block_order, col_share), 0) == iota((block_order, col_share), 1) + rows_start)
    )
    columns = columns_ref[...]
    left = jnp.zeros(left_ref.shape, f32)
    for s in range(replica_count):
        part = jnp.dot(block_ref[s], order, preferred_element_type=f32).astype(bf16)
        picked = jnp.dot(part, mine, preferred_element_type=f32).astype(bf16)
        left += lax.dot_general(
            picked, part, (((0,), (0,)), ((), ())), preferred_element_type=f32
        )
        right_ref[:, s * col_share : (s + 1) * col_share] = lax.dot_general(
            columns, block_ref[s], (((1,), (1,)), ((), ())), preferred_element_type=f32
        )
    left_ref[...] = left


def body(grad, owner, row_extent, col_extent, left_old, right_old, left_root, right_root):
    fsdp_count = lax.axis_size("fsdp")
    replica_count = lax.axis_size("replica")
    block_count, row_share, col_share = grad.shape
    block_order = row_share * fsdp_count
    lanes = wire_lanes(row_share, col_share)
    wire = pltpu.VMEM((fsdp_count, wire_halves, lanes), bf16)
    slots = pltpu.VMEM((lanes // lane_count, fsdp_count * wire_halves, lane_count), f32)
    owner_row, live_rows, live_cols = owner[None, :], row_extent[None, :], col_extent[None, :]
    turned_grad = grad.transpose(1, 0, 2)

    def exchange(sent):
        return lax.all_to_all(sent, "fsdp", split_axis=0, concat_axis=0, tiled=True)

    received = exchange(
        call(
            pack_kernel,
            wire,
            [hbm, hbm],
            "pack",
            2**20,
            [
                pltpu.VMEM(owner_row.shape, jnp.int32),
                pltpu.VMEM(turned_grad.shape, bf16),
                slots,
                pltpu.SemaphoreType.DMA((2,)),
            ],
        )(pltpu.with_memory_space_constraint(owner_row, pltpu.HBM),
          pltpu.with_memory_space_constraint(turned_grad, pltpu.HBM))
    )

    root_shape = (block_order, block_order)
    half = rounded_up(col_share, 16)
    left_high, left_low, right_pieces = call(
        functools.partial(prepare_kernel, row_share),
        [
            jax.ShapeDtypeStruct(root_shape, bf16),
            pltpu.HBM(root_shape, bf16),
            jax.ShapeDtypeStruct((replica_count, 2 * half, col_share), bf16),
        ],
        [vmem, vmem],
        "prepare",
        2**31,
        [pltpu.VMEM(root_shape, bf16), pltpu.SemaphoreType.DMA((1,))],
        [vmem, hbm, vmem],
    )(left_root[0], right_root[0])

    columns = call(
        functools.partial(turn_kernel, row_share),
        jax.ShapeDtypeStruct((col_share, block_order), bf16),
        [vmem] * 4,
        "turn",
        2**20,
        [slots],
    )(owner_row, live_rows, live_cols, received)
    block = lax.all_gather(columns, "replica", axis=0)
    result = call(
        functools.partial(update_kernel, row_share),
        wire,
        [vmem] * 6 + [hbm],
        "update",
        2**30,
        [slots, pltpu.VMEM(root_shape, bf16), pltpu.SemaphoreType.DMA((1,))],
    )(
        owner_row,
        live_rows,
        live_cols,
        block,
        right_pieces,
        left_high,
        pltpu.with_memory_space_constraint(left_low, pltpu.HBM),
    )
    returned = exchange(result)

    stat = jax.ShapeDtypeStruct((col_share, block_order), f32)
    left_rows, right_rows = call(
        functools.partial(stats_kernel, row_share),
        [stat, stat],
        [vmem, vmem, hbm],
        "stats",
        2**29,
    )(block, columns, result)
    left_new = decay_rate * left_old + ((1.0 - decay_rate) * left_rows)[None]
    right_new = decay_rate * right_old + ((1.0 - decay_rate) * right_rows)[None]

    update = call(
        unpack_kernel,
        jax.ShapeDtypeStruct((row_share, block_count, col_share), bf16),
        [vmem, vmem],
        "unpack",
        2**20,
        [slots],
    )(owner_row, returned)
    return (update.transpose(1, 0, 2), left_new, right_new)


def solution(mesh):
    placed = (
        P(None, "fsdp", "replica"),
        P(),
        P(),
        P(),
        P("fsdp", "replica", None),
        P("fsdp", "replica", None),
        P("fsdp", None, None),
        P("fsdp", "replica", None),
    )
    return jax.shard_map(
        body,
        mesh=mesh,
        in_specs=placed,
        out_specs=(
            P(None, "fsdp", "replica"),
            P("fsdp", "replica", None),
            P("fsdp", "replica", None),
        ),
        check_vma=False,
    )
```

```python
import functools

import jax
import jax.numpy as jnp
from jax import lax
from jax.experimental import pallas as pl
from jax.experimental.pallas import tpu as pltpu
from jax.sharding import PartitionSpec as P

decay_rate = 0.9
lane_count = 128
wire_halves = 2
f32 = jnp.float32
bf16 = jnp.bfloat16
vmem = pl.BlockSpec(memory_space=pltpu.VMEM)
hbm = pl.BlockSpec(memory_space=pltpu.HBM)


def call(kernel, out_shape, in_specs, name, flops, scratch=(), out_specs=None):
    return pl.pallas_call(
        kernel,
        out_shape=out_shape,
        in_specs=in_specs,
        out_specs=out_specs or jax.tree.map(lambda _: vmem, out_shape),
        scratch_shapes=list(scratch),
        compiler_params=pltpu.CompilerParams(vmem_limit_bytes=20 * 2**20),
        cost_estimate=pl.CostEstimate(flops=flops, bytes_accessed=2**20, transcendentals=0),
        name=name,
    )


def iota(shape, dim):
    return lax.broadcasted_iota(jnp.int32, shape, dim)


def rounded_up(value, step):
    return -(-value // step) * step


def one_hot(condition):
    return condition.astype(f32).astype(bf16)


def pitch_of(col_share):
    return rounded_up(col_share, 32)


def per_half_of(row_share):
    return -(-row_share // wire_halves)


def wire_lanes(row_share, col_share):
    return rounded_up(per_half_of(row_share) * pitch_of(col_share), lane_count)


def joined(pieces, lanes):
    rows = pieces[0].shape[0]
    width = sum(p.shape[1] for p in pieces)
    if width < lanes:
        pieces = [*pieces, jnp.zeros((rows, lanes - width), pieces[0].dtype)]
    return jnp.concatenate(pieces, axis=1)


def tiles(lanes):
    return [slice(t * lane_count, (t + 1) * lane_count) for t in range(lanes // lane_count)]


def put_half(slots, h, value):
    for t, part in enumerate(tiles(value.shape[1])):
        slots[t, pl.ds(h, value.shape[0], stride=wire_halves), :] = value[:, part]


def get_half(slots, h):
    count = (slots.shape[1] - 8) // wire_halves
    return jnp.concatenate(
        [slots[t, pl.ds(h, count, stride=wire_halves), :] for t in range(slots.shape[0])], axis=1
    )


def to_wire(slots, wire_ref):
    owners, halves, lanes = wire_ref.shape
    for t, part in enumerate(tiles(lanes)):
        rows = slots[t, : owners * halves].astype(bf16)
        wire_ref[:, :, part] = rows.reshape(owners, halves, lane_count)


def from_wire(slots, wire_ref):
    owners, halves, lanes = wire_ref.shape
    for t, part in enumerate(tiles(lanes)):
        rows = wire_ref[:, :, part].reshape(owners * halves, lane_count)
        slots[t, : owners * halves] = rows.astype(f32)


def pack_kernel(owner_hbm, grad_hbm, wire_ref, owner_ref, grad_ref, slots, sems):
    copies = [
        pltpu.make_async_copy(owner_hbm, owner_ref, sems.at[0]),
        pltpu.make_async_copy(grad_hbm, grad_ref, sems.at[1]),
    ]
    for copy in copies:
        copy.start()
    for copy in copies:
        copy.wait()
    row_share, block_count, col_share = grad_ref.shape
    fsdp_count, _, lanes = wire_ref.shape
    per_half = per_half_of(row_share)
    gap = jnp.zeros((block_count, pitch_of(col_share) - col_share), bf16)
    pick = one_hot(iota((fsdp_count, block_count), 0) == owner_ref[...])
    for h in range(wire_halves):
        pieces = []
        for i in range(h * per_half, min(row_share, (h + 1) * per_half)):
            pieces += [grad_ref[i], gap]
        put_half(
            slots, h, jnp.dot(pick, joined(pieces, lanes), preferred_element_type=f32)
        )
    to_wire(slots, wire_ref)


def unpack_kernel(owner_ref, wire_ref, update_ref, slots):
    row_share, block_count, col_share = update_ref.shape
    fsdp_count = wire_ref.shape[0]
    per_half = per_half_of(row_share)
    pitch = pitch_of(col_share)
    from_wire(slots, wire_ref)
    pick = one_hot(iota((fsdp_count, block_count), 0) == owner_ref[...])
    for h in range(wire_halves):
        rows = get_half(slots, h).astype(bf16)
        picked = lax.dot_general(pick, rows, (((0,), (0,)), ((), ())), preferred_element_type=f32)
        for i in range(h * per_half, min(row_share, (h + 1) * per_half)):
            start = (i - h * per_half) * pitch
            update_ref[i] = picked[:, start : start + col_share].astype(bf16)


def folded(columns):
    third = columns.shape[0] // 3
    middle = columns.shape[1] // 2
    rest = columns[2 * third :]
    rest = jnp.concatenate([rest[:, :middle], rest[:, middle:]], axis=0)
    return jnp.concatenate([columns[: 2 * third], rest], axis=1)


def order_matrix(row_share, fsdp_count, forward):
    parts = []
    for i in range(row_share):
        shape = (fsdp_count, row_share * fsdp_count)
        if not forward:
            shape = shape[::-1]
        place, index = (0, 1) if forward else (1, 0)
        parts.append(iota(shape, place) * row_share + i == iota(shape, index))
    parts = [one_hot(p) for p in parts]
    return jnp.concatenate(parts, axis=0 if forward else 1)


def prepare_kernel(
    row_share, left_ref, right_ref, left_high_ref, left_low_hbm, top_ref, rest_ref, left_low_ref,
    sem,
):
    block_order = left_ref.shape[0]
    fsdp_count = block_order // row_share
    rows = order_matrix(row_share, fsdp_count, True)
    cols = order_matrix(row_share, fsdp_count, False)
    left = left_ref[...]
    left_high = left.astype(bf16)
    left_low = (left - left_high.astype(f32)).astype(bf16)
    for part, ref in ((left_low, left_low_ref), (left_high, left_high_ref)):
        half_done = jnp.dot(rows, part, preferred_element_type=f32).astype(bf16)
        ref[...] = jnp.dot(half_done, cols, preferred_element_type=f32).astype(bf16)
    copy = pltpu.make_async_copy(left_low_ref, left_low_hbm, sem.at[0])
    copy.start()
    col_share = right_ref.shape[0]
    third = col_share // 3
    replica_count = block_order // col_share
    right = right_ref[...]
    right_high = right.astype(bf16).astype(f32)
    right_low = right - right_high
    filler = jnp.zeros((top_ref.shape[0] // 2 - col_share, block_order), f32)
    both = jnp.concatenate([right_high, filler, right_low, filler], axis=0)
    tops, uppers, lowers = [], [], []
    empty = jnp.zeros((both.shape[0], third), f32)
    for n in range(replica_count):
        start = n * col_share
        tops.append(both[:, start : start + 2 * third])
        rest = both[:, start + 2 * third : start + col_share]
        uppers += [rest, empty]
        lowers += [empty, rest]
    top_ref[...] = jnp.concatenate(tops, axis=1).astype(bf16)
    rest_ref[...] = jnp.concatenate(
        [jnp.concatenate(uppers, axis=1), jnp.concatenate(lowers, axis=1)], axis=0
    ).astype(bf16)
    copy.wait()


def owned_extent(owner_ref, extent_ref):
    mine = owner_ref[...] == lax.axis_index("fsdp")
    values = jnp.where(mine, extent_ref[...], 0).astype(f32)
    return jnp.sum(values, axis=1, keepdims=True).astype(jnp.int32)


def turn_kernel(
    row_share, owner_ref, rows_ref, cols_ref, wire_ref, columns_ref, folded_ref, slots
):
    col_share, block_order = columns_ref.shape
    fsdp_count = wire_ref.shape[0]
    per_half = per_half_of(row_share)
    pitch = pitch_of(col_share)
    live_rows = owned_extent(owner_ref, rows_ref)
    live_cols = owned_extent(owner_ref, cols_ref) - lax.axis_index("replica") * col_share
    from_wire(slots, wire_ref)
    shape = (col_share, fsdp_count)
    col_live = iota(shape, 0) < live_cols
    pieces = []
    for h in range(wire_halves):
        turned = get_half(slots, h).T
        for i in range(h * per_half, min(row_share, (h + 1) * per_half)):
            start = (i - h * per_half) * pitch
            keep = col_live & (iota(shape, 1) * row_share + i < live_rows)
            pieces.append(jnp.where(keep, turned[start : start + col_share], 0.0))
    columns = jnp.concatenate(pieces, axis=1)
    columns_ref[...] = columns.astype(bf16)
    folded_ref[...] = folded(columns).astype(bf16)


def update_kernel(
    row_share, col_share, owner_ref, rows_ref, cols_ref, block_ref, top_ref, rest_ref,
    left_high_ref, left_low_hbm, wire_ref, slots, left_low_ref, sem,
):
    copy = pltpu.make_async_copy(left_low_hbm, left_low_ref, sem.at[0])
    copy.start()
    block_order = left_high_ref.shape[0]
    fsdp_count = block_order // row_share
    per_half = per_half_of(row_share)
    pitch = pitch_of(col_share)
    half = top_ref.shape[0] // 2
    live_rows = owned_extent(owner_ref, rows_ref)
    live_cols = owned_extent(owner_ref, cols_ref) - lax.axis_index("replica") * col_share
    rest = jnp.dot(rest_ref[...], block_ref[:, block_order:], preferred_element_type=f32)
    rest = rest.reshape(4, half, rest.shape[1])
    total = jnp.dot(top_ref[...], block_ref[:, :block_order], preferred_element_type=f32)
    product = total[:half] + total[half:]
    product += jnp.concatenate([rest[0] + rest[1], rest[2] + rest[3]], axis=1)
    product = jnp.concatenate(
        [product, jnp.zeros((lane_count - half, block_order), f32)], axis=0
    )
    high = product.astype(bf16)
    low = (product - high.astype(f32)).astype(bf16)
    last = (((1,), (1,)), ((), ()))
    first = lax.dot_general(
        left_high_ref[...], jnp.concatenate([high, low], axis=0), last, preferred_element_type=f32
    )
    copy.wait()
    second = lax.dot_general(left_low_ref[...], high, last, preferred_element_type=f32)
    result = first[:, :lane_count] + first[:, lane_count:] + second
    shape = (fsdp_count, lane_count)
    lane = iota(shape, 1)
    col_live = (lane < live_cols) & (lane < col_share)
    for h in range(wire_halves):
        pieces = []
        for i in range(h * per_half, min(row_share, (h + 1) * per_half)):
            keep = col_live & (iota(shape, 0) * row_share + i < live_rows)
            piece = jnp.where(keep, result[i * fsdp_count : (i + 1) * fsdp_count], 0.0)
            pieces.append(piece[:, :pitch])
        put_half(slots, h, joined(pieces, wire_ref.shape[2]))
    to_wire(slots, wire_ref)


def stats_kernel(row_share, block_ref, columns_ref, after_ref, left_ref, right_ref):
    col_share, block_order = columns_ref.shape
    third = col_share // 3
    middle = block_order // 2
    replica_count = block_order // col_share
    order = order_matrix(row_share, block_order // row_share, True)
    rows_start = lax.axis_index("replica") * col_share
    mine = one_hot(
        iota((block_order, col_share), 0) == iota((block_order, col_share), 1) + rows_start
    )
    top = block_ref[:, :block_order]
    rest = block_ref[:, block_order:]
    natural_top = jnp.dot(top, order, preferred_element_type=f32).astype(bf16)
    split = (replica_count, 2 * third, block_order)
    upper = jnp.dot(rest, order[:middle], preferred_element_type=f32).reshape(split)
    lower = jnp.dot(rest, order[middle:], preferred_element_type=f32).reshape(split)
    columns = columns_ref[...]
    last = (((1,), (1,)), ((), ()))
    with_top = lax.dot_general(columns, top, last, preferred_element_type=f32)
    with_upper = lax.dot_general(columns[:, :middle], rest, last, preferred_element_type=f32)
    with_lower = lax.dot_general(columns[:, middle:], rest, last, preferred_element_type=f32)
    first = (((0,), (0,)), ((), ()))
    picked = jnp.dot(natural_top, mine, preferred_element_type=f32).astype(bf16)
    left = lax.dot_general(picked, natural_top, first, preferred_element_type=f32)
    for n in range(replica_count):
        natural = (upper[n, :third] + lower[n, third:]).astype(bf16)
        picked = jnp.dot(natural, mine, preferred_element_type=f32).astype(bf16)
        left += lax.dot_general(picked, natural, first, preferred_element_type=f32)
        start = n * col_share
        held = n * 2 * third
        right_ref[:, start : start + 2 * third] = with_top[:, held : held + 2 * third]
        right_ref[:, start + 2 * third : start + col_share] = (
            with_upper[:, held : held + third] + with_lower[:, held + third : held + 2 * third]
        )
    left_ref[...] = left


def body(grad, owner, row_extent, col_extent, left_old, right_old, left_root, right_root):
    fsdp_count = lax.axis_size("fsdp")
    replica_count = lax.axis_size("replica")
    block_count, row_share, col_share = grad.shape
    block_order = row_share * fsdp_count
    lanes = wire_lanes(row_share, col_share)
    wire = pltpu.VMEM((fsdp_count, wire_halves, lanes), bf16)
    slots = pltpu.VMEM((lanes // lane_count, fsdp_count * wire_halves + 8, lane_count), f32)
    owner_row, live_rows, live_cols = owner[None, :], row_extent[None, :], col_extent[None, :]
    turned_grad = grad.transpose(1, 0, 2)

    def exchange(sent):
        return lax.all_to_all(sent, "fsdp", split_axis=0, concat_axis=0, tiled=True)

    received = exchange(
        call(
            pack_kernel,
            wire,
            [hbm, hbm],
            "pack",
            2**20,
            [
                pltpu.VMEM(owner_row.shape, jnp.int32),
                pltpu.VMEM(turned_grad.shape, bf16),
                slots,
                pltpu.SemaphoreType.DMA((2,)),
            ],
        )(pltpu.with_memory_space_constraint(owner_row, pltpu.HBM),
          pltpu.with_memory_space_constraint(turned_grad, pltpu.HBM))
    )

    root_shape = (block_order, block_order)
    half = rounded_up(col_share, 16)
    folded_shape = (col_share // 3 * 2, block_order // 2 * 3)
    left_high, left_low, right_top, right_rest = call(
        functools.partial(prepare_kernel, row_share),
        [
            jax.ShapeDtypeStruct(root_shape, bf16),
            pltpu.HBM(root_shape, bf16),
            jax.ShapeDtypeStruct((2 * half, folded_shape[0] * replica_count), bf16),
            jax.ShapeDtypeStruct((4 * half, folded_shape[0] * replica_count), bf16),
        ],
        [vmem, vmem],
        "prepare",
        2**31,
        [pltpu.VMEM(root_shape, bf16), pltpu.SemaphoreType.DMA((1,))],
        [vmem, hbm, vmem, vmem],
    )(left_root[0], right_root[0])

    columns, sent = call(
        functools.partial(turn_kernel, row_share),
        [
            jax.ShapeDtypeStruct((col_share, block_order), bf16),
            jax.ShapeDtypeStruct(folded_shape, bf16),
        ],
        [vmem] * 4,
        "turn",
        2**20,
        [slots],
    )(owner_row, live_rows, live_cols, received)
    block = lax.all_gather(sent, "replica", axis=0, tiled=True)
    result = call(
        functools.partial(update_kernel, row_share, col_share),
        wire,
        [vmem] * 7 + [hbm],
        "update",
        2**30,
        [slots, pltpu.VMEM(root_shape, bf16), pltpu.SemaphoreType.DMA((1,))],
    )(
        owner_row,
        live_rows,
        live_cols,
        block,
        right_top,
        right_rest,
        left_high,
        pltpu.with_memory_space_constraint(left_low, pltpu.HBM),
    )
    returned = exchange(result)

    stat = jax.ShapeDtypeStruct((col_share, block_order), f32)
    left_rows, right_rows = call(
        functools.partial(stats_kernel, row_share),
        [stat, stat],
        [vmem, vmem, hbm],
        "stats",
        2**29,
    )(block, columns, result)
    left_new = decay_rate * left_old + ((1.0 - decay_rate) * left_rows)[None]
    right_new = decay_rate * right_old + ((1.0 - decay_rate) * right_rows)[None]

    update = call(
        unpack_kernel,
        jax.ShapeDtypeStruct((row_share, block_count, col_share), bf16),
        [vmem, vmem],
        "unpack",
        2**20,
        [slots],
    )(owner_row, returned)
    return (update.transpose(1, 0, 2), left_new, right_new)


def solution(mesh):
    placed = (
        P(None, "fsdp", "replica"),
        P(),
        P(),
        P(),
        P("fsdp", "replica", None),
        P("fsdp", "replica", None),
        P("fsdp", None, None),
        P("fsdp", "replica", None),
    )
    return jax.shard_map(
        body,
        mesh=mesh,
        in_specs=placed,
        out_specs=(
            P(None, "fsdp", "replica"),
            P("fsdp", "replica", None),
            P("fsdp", "replica", None),
        ),
        check_vma=False,
    )
```

```python
import functools

import jax
import jax.numpy as jnp
from jax import lax
from jax.experimental import pallas as pl
from jax.experimental.pallas import tpu as pltpu
from jax.sharding import PartitionSpec as P

decay_rate = 0.9
lane_count = 128
wire_halves = 2
f32 = jnp.float32
bf16 = jnp.bfloat16
vmem = pl.BlockSpec(memory_space=pltpu.VMEM)
hbm = pl.BlockSpec(memory_space=pltpu.HBM)


def call(kernel, out_shape, in_specs, name, flops, scratch=(), out_specs=None):
    return pl.pallas_call(
        kernel,
        out_shape=out_shape,
        in_specs=in_specs,
        out_specs=out_specs or jax.tree.map(lambda _: vmem, out_shape),
        scratch_shapes=list(scratch),
        compiler_params=pltpu.CompilerParams(vmem_limit_bytes=20 * 2**20),
        cost_estimate=pl.CostEstimate(flops=flops, bytes_accessed=2**20, transcendentals=0),
        name=name,
    )


def iota(shape, dim):
    return lax.broadcasted_iota(jnp.int32, shape, dim)


def rounded_up(value, step):
    return -(-value // step) * step


def one_hot(condition):
    return condition.astype(f32).astype(bf16)


def pitch_of(col_share):
    return rounded_up(col_share, 32)


def per_half_of(row_share):
    return -(-row_share // wire_halves)


def wire_lanes(row_share, col_share):
    return rounded_up(per_half_of(row_share) * pitch_of(col_share), lane_count)


def joined(pieces, lanes):
    rows = pieces[0].shape[0]
    width = sum(p.shape[1] for p in pieces)
    if width < lanes:
        pieces = [*pieces, jnp.zeros((rows, lanes - width), pieces[0].dtype)]
    return jnp.concatenate(pieces, axis=1)


def tiles(lanes):
    return [slice(t * lane_count, (t + 1) * lane_count) for t in range(lanes // lane_count)]


def put_half(slots, h, value):
    for t, part in enumerate(tiles(value.shape[1])):
        slots[t, pl.ds(h, value.shape[0], stride=wire_halves), :] = value[:, part]


def get_half(slots, h):
    count = (slots.shape[1] - 8) // wire_halves
    return jnp.concatenate(
        [slots[t, pl.ds(h, count, stride=wire_halves), :] for t in range(slots.shape[0])], axis=1
    )


def to_wire(slots, wire_ref):
    owners, halves, lanes = wire_ref.shape
    for t, part in enumerate(tiles(lanes)):
        rows = slots[t, : owners * halves].astype(bf16)
        wire_ref[:, :, part] = rows.reshape(owners, halves, lane_count)


def from_wire(slots, wire_ref):
    owners, halves, lanes = wire_ref.shape
    for t, part in enumerate(tiles(lanes)):
        rows = wire_ref[:, :, part].reshape(owners * halves, lane_count)
        slots[t, : owners * halves] = rows.astype(f32)


def pack_kernel(owner_hbm, grad_hbm, wire_ref, owner_ref, grad_ref, slots, sems):
    copies = [
        pltpu.make_async_copy(owner_hbm, owner_ref, sems.at[0]),
        pltpu.make_async_copy(grad_hbm, grad_ref, sems.at[1]),
    ]
    for copy in copies:
        copy.start()
    for copy in copies:
        copy.wait()
    row_share, block_count, col_share = grad_ref.shape
    fsdp_count, _, lanes = wire_ref.shape
    per_half = per_half_of(row_share)
    gap = jnp.zeros((block_count, pitch_of(col_share) - col_share), bf16)
    pick = one_hot(iota((fsdp_count, block_count), 0) == owner_ref[...])
    for h in range(wire_halves):
        pieces = []
        for i in range(h * per_half, min(row_share, (h + 1) * per_half)):
            pieces += [grad_ref[i], gap]
        put_half(
            slots, h, jnp.dot(pick, joined(pieces, lanes), preferred_element_type=f32)
        )
    to_wire(slots, wire_ref)


def unpack_kernel(owner_ref, wire_ref, update_ref, slots):
    row_share, block_count, col_share = update_ref.shape
    fsdp_count = wire_ref.shape[0]
    per_half = per_half_of(row_share)
    pitch = pitch_of(col_share)
    from_wire(slots, wire_ref)
    pick = one_hot(iota((fsdp_count, block_count), 0) == owner_ref[...])
    for h in range(wire_halves):
        rows = get_half(slots, h).astype(bf16)
        picked = lax.dot_general(pick, rows, (((0,), (0,)), ((), ())), preferred_element_type=f32)
        for i in range(h * per_half, min(row_share, (h + 1) * per_half)):
            start = (i - h * per_half) * pitch
            update_ref[i] = picked[:, start : start + col_share].astype(bf16)


def order_matrix(row_share, fsdp_count, forward):
    parts = []
    for i in range(row_share):
        shape = (fsdp_count, row_share * fsdp_count)
        if not forward:
            shape = shape[::-1]
        place, index = (0, 1) if forward else (1, 0)
        parts.append(iota(shape, place) * row_share + i == iota(shape, index))
    parts = [one_hot(p) for p in parts]
    return jnp.concatenate(parts, axis=0 if forward else 1)


def prepare_kernel(
    row_share, left_ref, right_ref, left_high_ref, left_low_hbm, pieces_ref, left_low_ref, sem
):
    block_order = left_ref.shape[0]
    fsdp_count = block_order // row_share
    rows = order_matrix(row_share, fsdp_count, True)
    cols = order_matrix(row_share, fsdp_count, False)
    left = left_ref[...]
    left_high = left.astype(bf16)
    left_low = (left - left_high.astype(f32)).astype(bf16)
    half_done = jnp.dot(rows, left_low, preferred_element_type=f32).astype(bf16)
    left_low_ref[...] = jnp.dot(half_done, cols, preferred_element_type=f32).astype(bf16)
    copy = pltpu.make_async_copy(left_low_ref, left_low_hbm, sem.at[0])
    copy.start()
    half_done = jnp.dot(rows, left_high, preferred_element_type=f32).astype(bf16)
    left_high_ref[...] = jnp.dot(half_done, cols, preferred_element_type=f32).astype(bf16)
    col_share = right_ref.shape[0]
    replica_count = block_order // col_share
    right = right_ref[...]
    right_high = right.astype(bf16).astype(f32)
    filler = jnp.zeros((pieces_ref.shape[0] // 2 - col_share, block_order), f32)
    both = jnp.concatenate([right_high, filler, right - right_high, filler], axis=0)
    gap = jnp.zeros((both.shape[0], pieces_ref.shape[1] // replica_count - col_share), f32)
    spaced = []
    for n in range(replica_count):
        spaced += [both[:, n * col_share : (n + 1) * col_share], gap]
    pieces_ref[...] = jnp.concatenate(spaced, axis=1).astype(bf16)
    copy.wait()


def owned_extent(owner_ref, extent_ref):
    mine = owner_ref[...] == lax.axis_index("fsdp")
    values = jnp.where(mine, extent_ref[...], 0).astype(f32)
    return jnp.sum(values, axis=1, keepdims=True).astype(jnp.int32)


def turn_kernel(row_share, col_share, owner_ref, rows_ref, cols_ref, wire_ref, columns_ref, slots):
    held_rows = columns_ref.shape[0]
    fsdp_count = wire_ref.shape[0]
    per_half = per_half_of(row_share)
    pitch = pitch_of(col_share)
    live_rows = owned_extent(owner_ref, rows_ref)
    live_cols = owned_extent(owner_ref, cols_ref) - lax.axis_index("replica") * col_share
    from_wire(slots, wire_ref)
    shape = (held_rows, fsdp_count)
    col_live = (iota(shape, 0) < live_cols) & (iota(shape, 0) < col_share)
    pieces = []
    for h in range(wire_halves):
        turned = get_half(slots, h).T
        for i in range(h * per_half, min(row_share, (h + 1) * per_half)):
            start = (i - h * per_half) * pitch
            keep = col_live & (iota(shape, 1) * row_share + i < live_rows)
            pieces.append(jnp.where(keep, turned[start : start + held_rows], 0.0))
    columns_ref[...] = jnp.concatenate(pieces, axis=1).astype(bf16)


def update_kernel(
    row_share, col_share, owner_ref, rows_ref, cols_ref, block_ref, right_ref, left_high_ref,
    left_low_hbm, wire_ref, slots, left_low_ref, sem,
):
    copy = pltpu.make_async_copy(left_low_hbm, left_low_ref, sem.at[0])
    copy.start()
    block_order = block_ref.shape[1]
    fsdp_count = block_order // row_share
    per_half = per_half_of(row_share)
    pitch = pitch_of(col_share)
    half = right_ref.shape[0] // 2
    live_rows = owned_extent(owner_ref, rows_ref)
    live_cols = owned_extent(owner_ref, cols_ref) - lax.axis_index("replica") * col_share
    total = jnp.dot(right_ref[...], block_ref[...], preferred_element_type=f32)
    product = total[:half] + total[half:]
    product = jnp.concatenate(
        [product, jnp.zeros((lane_count - half, block_order), f32)], axis=0
    )
    high = product.astype(bf16)
    low = (product - high.astype(f32)).astype(bf16)
    last = (((1,), (1,)), ((), ()))
    first = lax.dot_general(
        left_high_ref[...], jnp.concatenate([high, low], axis=0), last, preferred_element_type=f32
    )
    copy.wait()
    second = lax.dot_general(left_low_ref[...], high, last, preferred_element_type=f32)
    result = first[:, :lane_count] + first[:, lane_count:] + second
    shape = (fsdp_count, lane_count)
    lane = iota(shape, 1)
    col_live = (lane < live_cols) & (lane < col_share)
    for h in range(wire_halves):
        pieces = []
        for i in range(h * per_half, min(row_share, (h + 1) * per_half)):
            keep = col_live & (iota(shape, 0) * row_share + i < live_rows)
            piece = jnp.where(keep, result[i * fsdp_count : (i + 1) * fsdp_count], 0.0)
            pieces.append(piece[:, :pitch])
        put_half(slots, h, joined(pieces, wire_ref.shape[2]))
    to_wire(slots, wire_ref)


def stats_kernel(row_share, col_share, block_ref, columns_ref, after_ref, left_ref, right_ref):
    held_rows, block_order = columns_ref.shape
    order = order_matrix(row_share, block_order // row_share, True)
    rows_start = lax.axis_index("replica") * col_share
    shape = (block_order, col_share)
    mine = one_hot(iota(shape, 0) == iota(shape, 1) + rows_start)
    natural = jnp.dot(block_ref[...], order, preferred_element_type=f32).astype(bf16)
    picked = jnp.dot(natural, mine, preferred_element_type=f32).astype(bf16)
    left_ref[...] = lax.dot_general(
        picked, natural, (((0,), (0,)), ((), ())), preferred_element_type=f32
    )
    right = lax.dot_general(
        columns_ref[...], block_ref[...], (((1,), (1,)), ((), ())), preferred_element_type=f32
    )[:col_share]
    for n in range(block_order // col_share):
        held = right[:, n * held_rows : n * held_rows + col_share]
        right_ref[:, n * col_share : (n + 1) * col_share] = held


def body(grad, owner, row_extent, col_extent, left_old, right_old, left_root, right_root):
    fsdp_count = lax.axis_size("fsdp")
    replica_count = lax.axis_size("replica")
    block_count, row_share, col_share = grad.shape
    block_order = row_share * fsdp_count
    lanes = wire_lanes(row_share, col_share)
    wire = pltpu.VMEM((fsdp_count, wire_halves, lanes), bf16)
    slots = pltpu.VMEM((lanes // lane_count, fsdp_count * wire_halves + 8, lane_count), f32)
    owner_row, live_rows, live_cols = owner[None, :], row_extent[None, :], col_extent[None, :]
    turned_grad = grad.transpose(1, 0, 2)

    def exchange(sent):
        return lax.all_to_all(sent, "fsdp", split_axis=0, concat_axis=0, tiled=True)

    received = exchange(
        call(
            pack_kernel,
            wire,
            [hbm, hbm],
            "pack",
            2**20,
            [
                pltpu.VMEM(owner_row.shape, jnp.int32),
                pltpu.VMEM(turned_grad.shape, bf16),
                slots,
                pltpu.SemaphoreType.DMA((2,)),
            ],
        )(pltpu.with_memory_space_constraint(owner_row, pltpu.HBM),
          pltpu.with_memory_space_constraint(turned_grad, pltpu.HBM))
    )

    root_shape = (block_order, block_order)
    half = rounded_up(col_share, 16)
    held_rows = rounded_up(col_share, 8)
    left_high, left_low, right_pieces = call(
        functools.partial(prepare_kernel, row_share),
        [
            jax.ShapeDtypeStruct(root_shape, bf16),
            pltpu.HBM(root_shape, bf16),
            jax.ShapeDtypeStruct((2 * half, replica_count * held_rows), bf16),
        ],
        [vmem, vmem],
        "prepare",
        2**31,
        [pltpu.VMEM(root_shape, bf16), pltpu.SemaphoreType.DMA((1,))],
        [vmem, hbm, vmem],
    )(left_root[0], right_root[0])

    columns = call(
        functools.partial(turn_kernel, row_share, col_share),
        jax.ShapeDtypeStruct((held_rows, block_order), bf16),
        [vmem] * 4,
        "turn",
        2**20,
        [slots],
    )(owner_row, live_rows, live_cols, received)
    block = lax.all_gather(columns, "replica", axis=0, tiled=True)
    result = call(
        functools.partial(update_kernel, row_share, col_share),
        wire,
        [vmem] * 6 + [hbm],
        "update",
        2**30,
        [slots, pltpu.VMEM(root_shape, bf16), pltpu.SemaphoreType.DMA((1,))],
    )(
        owner_row,
        live_rows,
        live_cols,
        block,
        right_pieces,
        left_high,
        pltpu.with_memory_space_constraint(left_low, pltpu.HBM),
    )
    returned = exchange(result)

    stat = jax.ShapeDtypeStruct((col_share, block_order), f32)
    left_rows, right_rows = call(
        functools.partial(stats_kernel, row_share, col_share),
        [stat, stat],
        [vmem, vmem, hbm],
        "stats",
        2**29,
    )(block, columns, result)
    left_new = decay_rate * left_old + ((1.0 - decay_rate) * left_rows)[None]
    right_new = decay_rate * right_old + ((1.0 - decay_rate) * right_rows)[None]

    update = call(
        unpack_kernel,
        jax.ShapeDtypeStruct((row_share, block_count, col_share), bf16),
        [vmem, vmem],
        "unpack",
        2**20,
        [slots],
    )(owner_row, returned)
    return (update.transpose(1, 0, 2), left_new, right_new)


def solution(mesh):
    placed = (
        P(None, "fsdp", "replica"),
        P(),
        P(),
        P(),
        P("fsdp", "replica", None),
        P("fsdp", "replica", None),
        P("fsdp", None, None),
        P("fsdp", "replica", None),
    )
    return jax.shard_map(
        body,
        mesh=mesh,
        in_specs=placed,
        out_specs=(
            P(None, "fsdp", "replica"),
            P("fsdp", "replica", None),
            P("fsdp", "replica", None),
        ),
        check_vma=False,
    )
```

```python
import functools

import jax
import jax.numpy as jnp
from jax import lax
from jax.experimental import pallas as pl
from jax.experimental.pallas import tpu as pltpu
from jax.sharding import PartitionSpec as P

decay_rate = 0.9
lane_count = 128
wire_halves = 2
f32 = jnp.float32
bf16 = jnp.bfloat16
vmem = pl.BlockSpec(memory_space=pltpu.VMEM)
hbm = pl.BlockSpec(memory_space=pltpu.HBM)


def call(kernel, out_shape, in_specs, name, flops, scratch=(), out_specs=None):
    return pl.pallas_call(
        kernel,
        out_shape=out_shape,
        in_specs=in_specs,
        out_specs=out_specs or jax.tree.map(lambda _: vmem, out_shape),
        scratch_shapes=list(scratch),
        compiler_params=pltpu.CompilerParams(vmem_limit_bytes=20 * 2**20),
        cost_estimate=pl.CostEstimate(flops=flops, bytes_accessed=2**20, transcendentals=0),
        name=name,
    )


def iota(shape, dim):
    return lax.broadcasted_iota(jnp.int32, shape, dim)


def rounded_up(value, step):
    return -(-value // step) * step


def one_hot(condition):
    return condition.astype(f32).astype(bf16)


def pitch_of(col_share):
    return rounded_up(col_share, 32)


def per_half_of(row_share):
    return -(-row_share // wire_halves)


def wire_lanes(row_share, col_share):
    return rounded_up(per_half_of(row_share) * pitch_of(col_share), lane_count)


def joined(pieces, lanes):
    rows = pieces[0].shape[0]
    width = sum(p.shape[1] for p in pieces)
    if width < lanes:
        pieces = [*pieces, jnp.zeros((rows, lanes - width), pieces[0].dtype)]
    return jnp.concatenate(pieces, axis=1)


def tiles(lanes):
    return [slice(t * lane_count, (t + 1) * lane_count) for t in range(lanes // lane_count)]


def put_half(slots, h, value):
    for t, part in enumerate(tiles(value.shape[1])):
        slots[t, pl.ds(h, value.shape[0], stride=wire_halves), :] = value[:, part]


def get_half(slots, h):
    count = (slots.shape[1] - 8) // wire_halves
    return jnp.concatenate(
        [slots[t, pl.ds(h, count, stride=wire_halves), :] for t in range(slots.shape[0])], axis=1
    )


def to_wire(slots, wire_ref):
    owners, halves, lanes = wire_ref.shape
    for t, part in enumerate(tiles(lanes)):
        rows = slots[t, : owners * halves].astype(bf16)
        wire_ref[:, :, part] = rows.reshape(owners, halves, lane_count)


def from_wire(slots, wire_ref):
    owners, halves, lanes = wire_ref.shape
    for t, part in enumerate(tiles(lanes)):
        rows = wire_ref[:, :, part].reshape(owners * halves, lane_count)
        slots[t, : owners * halves] = rows.astype(f32)


def pack_kernel(owner_hbm, grad_hbm, wire_ref, owner_ref, grad_ref, slots, sems):
    copies = [
        pltpu.make_async_copy(owner_hbm, owner_ref, sems.at[0]),
        pltpu.make_async_copy(grad_hbm, grad_ref, sems.at[1]),
    ]
    for copy in copies:
        copy.start()
    for copy in copies:
        copy.wait()
    row_share, block_count, col_share = grad_ref.shape
    fsdp_count, _, lanes = wire_ref.shape
    per_half = per_half_of(row_share)
    gap = jnp.zeros((block_count, pitch_of(col_share) - col_share), bf16)
    pick = one_hot(iota((fsdp_count, block_count), 0) == owner_ref[...])
    for h in range(wire_halves):
        pieces = []
        for i in range(h * per_half, min(row_share, (h + 1) * per_half)):
            pieces += [grad_ref[i], gap]
        put_half(
            slots, h, jnp.dot(pick, joined(pieces, lanes), preferred_element_type=f32)
        )
    to_wire(slots, wire_ref)


def unpack_kernel(owner_ref, wire_ref, update_ref, slots):
    row_share, block_count, col_share = update_ref.shape
    fsdp_count = wire_ref.shape[0]
    per_half = per_half_of(row_share)
    pitch = pitch_of(col_share)
    from_wire(slots, wire_ref)
    pick = one_hot(iota((fsdp_count, block_count), 0) == owner_ref[...])
    for h in range(wire_halves):
        rows = get_half(slots, h).astype(bf16)
        picked = lax.dot_general(pick, rows, (((0,), (0,)), ((), ())), preferred_element_type=f32)
        for i in range(h * per_half, min(row_share, (h + 1) * per_half)):
            start = (i - h * per_half) * pitch
            update_ref[i] = picked[:, start : start + col_share].astype(bf16)


def folded(columns, col_share):
    quarter = col_share // 4
    wide = columns.shape[1]
    piece = wide // 3
    rest = columns[3 * quarter : col_share]
    rest = [rest[:, t * piece : (t + 1) * piece] for t in range(3)]
    empty = rounded_up(3 * quarter, 16) - 3 * quarter
    top = jnp.concatenate([columns[: 3 * quarter], jnp.zeros((empty, wide), f32)], axis=0)
    rest = jnp.concatenate([*rest, jnp.zeros((empty, piece), f32)], axis=0)
    return jnp.concatenate([top, rest], axis=1)


def order_matrix(row_share, fsdp_count, forward):
    parts = []
    for i in range(row_share):
        shape = (fsdp_count, row_share * fsdp_count)
        if not forward:
            shape = shape[::-1]
        place, index = (0, 1) if forward else (1, 0)
        parts.append(iota(shape, place) * row_share + i == iota(shape, index))
    parts = [one_hot(p) for p in parts]
    return jnp.concatenate(parts, axis=0 if forward else 1)


def prepare_kernel(
    row_share, left_ref, right_ref, left_high_ref, left_low_hbm, pieces_ref, left_low_ref, sem
):
    block_order = left_ref.shape[0]
    fsdp_count = block_order // row_share
    rows = order_matrix(row_share, fsdp_count, True)
    cols = order_matrix(row_share, fsdp_count, False)
    left = left_ref[...]
    left_high = left.astype(bf16)
    left_low = (left - left_high.astype(f32)).astype(bf16)
    half_done = jnp.dot(rows, left_low, preferred_element_type=f32).astype(bf16)
    left_low_ref[...] = jnp.dot(half_done, cols, preferred_element_type=f32).astype(bf16)
    copy = pltpu.make_async_copy(left_low_ref, left_low_hbm, sem.at[0])
    copy.start()
    half_done = jnp.dot(rows, left_high, preferred_element_type=f32).astype(bf16)
    left_high_ref[...] = jnp.dot(half_done, cols, preferred_element_type=f32).astype(bf16)
    col_share = right_ref.shape[0]
    replica_count = block_order // col_share
    right = right_ref[...]
    right_high = right.astype(bf16).astype(f32)
    filler = jnp.zeros((pieces_ref.shape[0] // 8 - col_share, block_order), f32)
    both = jnp.concatenate([right_high, filler, right - right_high, filler], axis=0)
    quarter = col_share // 4
    held_rows = pieces_ref.shape[1] // replica_count

    def blank(count):
        return jnp.zeros((both.shape[0], count), f32)

    spaced = []
    for n in range(replica_count):
        start = n * col_share
        spaced += [both[:, start : start + 3 * quarter], blank(held_rows - 3 * quarter)]
    pieces_ref[: both.shape[0]] = jnp.concatenate(spaced, axis=1).astype(bf16)
    for t in range(3):
        spaced = []
        for n in range(replica_count):
            start = n * col_share + 3 * quarter
            if t:
                spaced.append(blank(t * quarter))
            spaced += [both[:, start : start + quarter], blank(held_rows - (t + 1) * quarter)]
        held = slice((t + 1) * both.shape[0], (t + 2) * both.shape[0])
        pieces_ref[held] = jnp.concatenate(spaced, axis=1).astype(bf16)
    copy.wait()


def owned_extent(owner_ref, extent_ref):
    mine = owner_ref[...] == lax.axis_index("fsdp")
    values = jnp.where(mine, extent_ref[...], 0).astype(f32)
    return jnp.sum(values, axis=1, keepdims=True).astype(jnp.int32)


def turn_kernel(row_share, col_share, owner_ref, rows_ref, cols_ref, wire_ref, columns_ref, folded_ref, slots):
    held_rows = columns_ref.shape[0]
    fsdp_count = wire_ref.shape[0]
    per_half = per_half_of(row_share)
    pitch = pitch_of(col_share)
    live_rows = owned_extent(owner_ref, rows_ref)
    live_cols = owned_extent(owner_ref, cols_ref) - lax.axis_index("replica") * col_share
    from_wire(slots, wire_ref)
    shape = (held_rows, fsdp_count)
    col_live = (iota(shape, 0) < live_cols) & (iota(shape, 0) < col_share)
    pieces = []
    for h in range(wire_halves):
        turned = get_half(slots, h).T
        for i in range(h * per_half, min(row_share, (h + 1) * per_half)):
            start = (i - h * per_half) * pitch
            keep = col_live & (iota(shape, 1) * row_share + i < live_rows)
            pieces.append(jnp.where(keep, turned[start : start + held_rows], 0.0))
    columns = jnp.concatenate(pieces, axis=1)
    columns_ref[...] = columns.astype(bf16)
    folded_ref[...] = folded(columns, col_share).astype(bf16)


def update_kernel(
    row_share, col_share, owner_ref, rows_ref, cols_ref, block_ref, right_ref, left_high_ref,
    left_low_hbm, wire_ref, slots, left_low_ref, sem,
):
    copy = pltpu.make_async_copy(left_low_hbm, left_low_ref, sem.at[0])
    copy.start()
    block_order = left_high_ref.shape[0]
    fsdp_count = block_order // row_share
    per_half = per_half_of(row_share)
    pitch = pitch_of(col_share)
    half = right_ref.shape[0] // 8
    live_rows = owned_extent(owner_ref, rows_ref)
    live_cols = owned_extent(owner_ref, cols_ref) - lax.axis_index("replica") * col_share
    whole = block_order // lane_count * lane_count
    rest = jnp.dot(right_ref[2 * half :], block_ref[:, whole:], preferred_element_type=f32)
    rest = rest[:, block_order - whole :].reshape(3, 2, half, block_order // 3)
    total = jnp.dot(
        right_ref[: 2 * half], block_ref[:, :block_order], preferred_element_type=f32
    )
    product = total[:half] + total[half:]
    product += jnp.concatenate([rest[t, 0] + rest[t, 1] for t in range(3)], axis=1)
    product = jnp.concatenate(
        [product, jnp.zeros((lane_count - half, block_order), f32)], axis=0
    )
    high = product.astype(bf16)
    low = (product - high.astype(f32)).astype(bf16)
    last = (((1,), (1,)), ((), ()))
    first = lax.dot_general(
        left_high_ref[...], jnp.concatenate([high, low], axis=0), last, preferred_element_type=f32
    )
    copy.wait()
    second = lax.dot_general(left_low_ref[...], high, last, preferred_element_type=f32)
    result = first[:, :lane_count] + first[:, lane_count:] + second
    shape = (fsdp_count, lane_count)
    lane = iota(shape, 1)
    col_live = (lane < live_cols) & (lane < col_share)
    for h in range(wire_halves):
        pieces = []
        for i in range(h * per_half, min(row_share, (h + 1) * per_half)):
            keep = col_live & (iota(shape, 0) * row_share + i < live_rows)
            piece = jnp.where(keep, result[i * fsdp_count : (i + 1) * fsdp_count], 0.0)
            pieces.append(piece[:, :pitch])
        put_half(slots, h, joined(pieces, wire_ref.shape[2]))
    to_wire(slots, wire_ref)


def stats_kernel(row_share, col_share, block_ref, columns_ref, after_ref, left_ref, right_ref):
    held_rows, block_order = columns_ref.shape
    order = order_matrix(row_share, block_order // row_share, True)
    rows_start = lax.axis_index("replica") * col_share
    shape = (block_order, col_share)
    mine = one_hot(iota(shape, 0) == iota(shape, 1) + rows_start)
    replica_count = block_order // col_share
    quarter = col_share // 4
    piece = block_order // 3
    held_rows = block_ref.shape[0] // replica_count
    top = block_ref[:, :block_order]
    rest = block_ref[:, block_order:]
    columns = columns_ref[...]
    last = (((1,), (1,)), ((), ()))
    first = (((0,), (0,)), ((), ()))
    with_top = lax.dot_general(columns, top, last, preferred_element_type=f32)
    natural_rest, with_rest = [], []
    for t in range(3):
        held = slice(t * piece, (t + 1) * piece)
        natural_rest.append(jnp.dot(rest, order[held], preferred_element_type=f32))
        with_rest.append(
            lax.dot_general(columns[:, held], rest, last, preferred_element_type=f32)
        )
    natural = jnp.dot(top, order, preferred_element_type=f32).astype(bf16)
    picked = jnp.dot(natural, mine, preferred_element_type=f32).astype(bf16)
    left = lax.dot_general(picked, natural, first, preferred_element_type=f32)
    for n in range(replica_count):
        held = [n * held_rows + t * quarter for t in range(3)]
        natural = sum(natural_rest[t][held[t] : held[t] + quarter] for t in range(3)).astype(bf16)
        picked = jnp.dot(natural, mine, preferred_element_type=f32).astype(bf16)
        left += lax.dot_general(picked, natural, first, preferred_element_type=f32)
        start = n * col_share
        right_ref[:, start : start + 3 * quarter] = with_top[
            :col_share, n * held_rows : n * held_rows + 3 * quarter
        ]
        right_ref[:, start + 3 * quarter : start + col_share] = sum(
            with_rest[t][:col_share, held[t] : held[t] + quarter] for t in range(3)
        )
    left_ref[...] = left


def body(grad, owner, row_extent, col_extent, left_old, right_old, left_root, right_root):
    fsdp_count = lax.axis_size("fsdp")
    replica_count = lax.axis_size("replica")
    block_count, row_share, col_share = grad.shape
    block_order = row_share * fsdp_count
    lanes = wire_lanes(row_share, col_share)
    wire = pltpu.VMEM((fsdp_count, wire_halves, lanes), bf16)
    slots = pltpu.VMEM((lanes // lane_count, fsdp_count * wire_halves + 8, lane_count), f32)
    owner_row, live_rows, live_cols = owner[None, :], row_extent[None, :], col_extent[None, :]
    turned_grad = grad.transpose(1, 0, 2)

    def exchange(sent):
        return lax.all_to_all(sent, "fsdp", split_axis=0, concat_axis=0, tiled=True)

    received = exchange(
        call(
            pack_kernel,
            wire,
            [hbm, hbm],
            "pack",
            2**20,
            [
                pltpu.VMEM(owner_row.shape, jnp.int32),
                pltpu.VMEM(turned_grad.shape, bf16),
                slots,
                pltpu.SemaphoreType.DMA((2,)),
            ],
        )(pltpu.with_memory_space_constraint(owner_row, pltpu.HBM),
          pltpu.with_memory_space_constraint(turned_grad, pltpu.HBM))
    )

    root_shape = (block_order, block_order)
    half = rounded_up(col_share, 16)
    held_rows = rounded_up(col_share, 8)
    folded_shape = (rounded_up(col_share // 4 * 3, 16), block_order // 3 * 4)
    left_high, left_low, right_pieces = call(
        functools.partial(prepare_kernel, row_share),
        [
            jax.ShapeDtypeStruct(root_shape, bf16),
            pltpu.HBM(root_shape, bf16),
            jax.ShapeDtypeStruct((8 * half, replica_count * folded_shape[0]), bf16),
        ],
        [vmem, vmem],
        "prepare",
        2**31,
        [pltpu.VMEM(root_shape, bf16), pltpu.SemaphoreType.DMA((1,))],
        [vmem, hbm, vmem],
    )(left_root[0], right_root[0])

    columns, sent = call(
        functools.partial(turn_kernel, row_share, col_share),
        [
            jax.ShapeDtypeStruct((held_rows, block_order), bf16),
            jax.ShapeDtypeStruct(folded_shape, bf16),
        ],
        [vmem] * 4,
        "turn",
        2**20,
        [slots],
    )(owner_row, live_rows, live_cols, received)
    block = lax.all_gather(sent, "replica", axis=0, tiled=True)
    result = call(
        functools.partial(update_kernel, row_share, col_share),
        wire,
        [vmem] * 6 + [hbm],
        "update",
        2**30,
        [slots, pltpu.VMEM(root_shape, bf16), pltpu.SemaphoreType.DMA((1,))],
    )(
        owner_row,
        live_rows,
        live_cols,
        block,
        right_pieces,
        left_high,
        pltpu.with_memory_space_constraint(left_low, pltpu.HBM),
    )
    returned = exchange(result)

    stat = jax.ShapeDtypeStruct((col_share, block_order), f32)
    left_rows, right_rows = call(
        functools.partial(stats_kernel, row_share, col_share),
        [stat, stat],
        [vmem, vmem, hbm],
        "stats",
        2**29,
    )(block, columns, result)
    left_new = decay_rate * left_old + ((1.0 - decay_rate) * left_rows)[None]
    right_new = decay_rate * right_old + ((1.0 - decay_rate) * right_rows)[None]

    update = call(
        unpack_kernel,
        jax.ShapeDtypeStruct((row_share, block_count, col_share), bf16),
        [vmem, vmem],
        "unpack",
        2**20,
        [slots],
    )(owner_row, returned)
    return (update.transpose(1, 0, 2), left_new, right_new)


def solution(mesh):
    placed = (
        P(None, "fsdp", "replica"),
        P(),
        P(),
        P(),
        P("fsdp", "replica", None),
        P("fsdp", "replica", None),
        P("fsdp", None, None),
        P("fsdp", "replica", None),
    )
    return jax.shard_map(
        body,
        mesh=mesh,
        in_specs=placed,
        out_specs=(
            P(None, "fsdp", "replica"),
            P("fsdp", "replica", None),
            P("fsdp", "replica", None),
        ),
        check_vma=False,
    )
```

```python
import functools

import jax
import jax.numpy as jnp
from jax import lax
from jax.experimental import pallas as pl
from jax.experimental.pallas import tpu as pltpu
from jax.sharding import PartitionSpec as P

decay_rate = 0.9
lane_count = 128
wire_halves = 2
send_parts = 2
f32 = jnp.float32
bf16 = jnp.bfloat16
vmem = pl.BlockSpec(memory_space=pltpu.VMEM)
hbm = pl.BlockSpec(memory_space=pltpu.HBM)


def call(kernel, out_shape, in_specs, name, flops, scratch=(), out_specs=None):
    return pl.pallas_call(
        kernel,
        out_shape=out_shape,
        in_specs=in_specs,
        out_specs=out_specs or jax.tree.map(lambda _: vmem, out_shape),
        scratch_shapes=list(scratch),
        compiler_params=pltpu.CompilerParams(vmem_limit_bytes=20 * 2**20),
        cost_estimate=pl.CostEstimate(flops=flops, bytes_accessed=2**20, transcendentals=0),
        name=name,
    )


def iota(shape, dim):
    return lax.broadcasted_iota(jnp.int32, shape, dim)


def rounded_up(value, step):
    return -(-value // step) * step


def one_hot(condition):
    return condition.astype(f32).astype(bf16)


def pitch_of(col_share):
    return rounded_up(col_share, 32)


def per_half_of(row_share):
    return -(-row_share // wire_halves)


def wire_lanes(row_share, col_share):
    return rounded_up(per_half_of(row_share) * pitch_of(col_share), lane_count)


def joined(pieces, lanes):
    rows = pieces[0].shape[0]
    width = sum(p.shape[1] for p in pieces)
    if width < lanes:
        pieces = [*pieces, jnp.zeros((rows, lanes - width), pieces[0].dtype)]
    return jnp.concatenate(pieces, axis=1)


def tiles(lanes):
    return [slice(t * lane_count, (t + 1) * lane_count) for t in range(lanes // lane_count)]


def put_half(slots, h, value):
    for t, part in enumerate(tiles(value.shape[1])):
        slots[t, pl.ds(h, value.shape[0], stride=wire_halves), :] = value[:, part]


def get_half(slots, h):
    count = (slots.shape[1] - 8) // wire_halves
    return jnp.concatenate(
        [slots[t, pl.ds(h, count, stride=wire_halves), :] for t in range(slots.shape[0])], axis=1
    )


def to_wire(slots, wire_ref):
    owners, halves, lanes = wire_ref.shape
    for t, part in enumerate(tiles(lanes)):
        rows = slots[t, : owners * halves].astype(bf16)
        wire_ref[:, :, part] = rows.reshape(owners, halves, lane_count)


def from_wire(slots, wire_ref):
    owners, halves, lanes = wire_ref.shape
    for t, part in enumerate(tiles(lanes)):
        rows = wire_ref[:, :, part].reshape(owners * halves, lane_count)
        slots[t, : owners * halves] = rows.astype(f32)


def pack_kernel(owner_hbm, grad_hbm, wire_ref, owner_ref, grad_ref, slots, sems):
    copies = [
        pltpu.make_async_copy(owner_hbm, owner_ref, sems.at[0]),
        pltpu.make_async_copy(grad_hbm, grad_ref, sems.at[1]),
    ]
    for copy in copies:
        copy.start()
    for copy in copies:
        copy.wait()
    row_share, block_count, col_share = grad_ref.shape
    fsdp_count, _, lanes = wire_ref.shape
    per_half = per_half_of(row_share)
    gap = jnp.zeros((block_count, pitch_of(col_share) - col_share), bf16)
    pick = one_hot(iota((fsdp_count, block_count), 0) == owner_ref[...])
    for h in range(wire_halves):
        pieces = []
        for i in range(h * per_half, min(row_share, (h + 1) * per_half)):
            pieces += [grad_ref[i], gap]
        put_half(
            slots, h, jnp.dot(pick, joined(pieces, lanes), preferred_element_type=f32)
        )
    to_wire(slots, wire_ref)


def unpack_kernel(owner_ref, wire_ref, update_ref, slots):
    row_share, block_count, col_share = update_ref.shape
    fsdp_count = wire_ref.shape[0]
    per_half = per_half_of(row_share)
    pitch = pitch_of(col_share)
    from_wire(slots, wire_ref)
    pick = one_hot(iota((fsdp_count, block_count), 0) == owner_ref[...])
    for h in range(wire_halves):
        rows = get_half(slots, h).astype(bf16)
        picked = lax.dot_general(pick, rows, (((0,), (0,)), ((), ())), preferred_element_type=f32)
        for i in range(h * per_half, min(row_share, (h + 1) * per_half)):
            start = (i - h * per_half) * pitch
            update_ref[i] = picked[:, start : start + col_share].astype(bf16)


def folded(columns, col_share):
    quarter = col_share // 4
    wide = columns.shape[1]
    piece = wide // 3
    rest = columns[3 * quarter : col_share]
    rest = [rest[:, t * piece : (t + 1) * piece] for t in range(3)]
    empty = rounded_up(3 * quarter, 16) - 3 * quarter
    top = jnp.concatenate([columns[: 3 * quarter], jnp.zeros((empty, wide), f32)], axis=0)
    rest = jnp.concatenate([*rest, jnp.zeros((empty, piece), f32)], axis=0)
    return jnp.concatenate([top, rest], axis=1)


def order_matrix(row_share, fsdp_count, forward):
    parts = []
    for i in range(row_share):
        shape = (fsdp_count, row_share * fsdp_count)
        if not forward:
            shape = shape[::-1]
        place, index = (0, 1) if forward else (1, 0)
        parts.append(iota(shape, place) * row_share + i == iota(shape, index))
    parts = [one_hot(p) for p in parts]
    return jnp.concatenate(parts, axis=0 if forward else 1)


def wire_order_matrix(row_share, fsdp_count):
    count = fsdp_count // send_parts
    shape = (count, row_share * fsdp_count)
    parts = []
    for q in range(send_parts):
        for i in range(row_share):
            parts.append(one_hot((iota(shape, 0) + q * count) * row_share + i == iota(shape, 1)))
    return jnp.concatenate(parts, axis=0)


def prepare_kernel(
    row_share, left_ref, right_ref, left_high_ref, left_low_hbm, pieces_ref, left_low_ref, sem
):
    block_order = left_ref.shape[0]
    fsdp_count = block_order // row_share
    rows = wire_order_matrix(row_share, fsdp_count)
    cols = order_matrix(row_share, fsdp_count, False)
    left = left_ref[...]
    left_high = left.astype(bf16)
    left_low = (left - left_high.astype(f32)).astype(bf16)
    half_done = jnp.dot(rows, left_low, preferred_element_type=f32).astype(bf16)
    left_low_ref[...] = jnp.dot(half_done, cols, preferred_element_type=f32).astype(bf16)
    copy = pltpu.make_async_copy(left_low_ref, left_low_hbm, sem.at[0])
    copy.start()
    half_done = jnp.dot(rows, left_high, preferred_element_type=f32).astype(bf16)
    left_high_ref[...] = jnp.dot(half_done, cols, preferred_element_type=f32).astype(bf16)
    col_share = right_ref.shape[0]
    replica_count = block_order // col_share
    right = right_ref[...]
    right_high = right.astype(bf16).astype(f32)
    filler = jnp.zeros((pieces_ref.shape[0] // 8 - col_share, block_order), f32)
    both = jnp.concatenate([right_high, filler, right - right_high, filler], axis=0)
    quarter = col_share // 4
    held_rows = pieces_ref.shape[1] // replica_count

    def blank(count):
        return jnp.zeros((both.shape[0], count), f32)

    spaced = []
    for n in range(replica_count):
        start = n * col_share
        spaced += [both[:, start : start + 3 * quarter], blank(held_rows - 3 * quarter)]
    pieces_ref[: both.shape[0]] = jnp.concatenate(spaced, axis=1).astype(bf16)
    for t in range(3):
        spaced = []
        for n in range(replica_count):
            start = n * col_share + 3 * quarter
            if t:
                spaced.append(blank(t * quarter))
            spaced += [both[:, start : start + quarter], blank(held_rows - (t + 1) * quarter)]
        held = slice((t + 1) * both.shape[0], (t + 2) * both.shape[0])
        pieces_ref[held] = jnp.concatenate(spaced, axis=1).astype(bf16)
    copy.wait()


def owned_extent(owner_ref, extent_ref):
    mine = owner_ref[...] == lax.axis_index("fsdp")
    values = jnp.where(mine, extent_ref[...], 0).astype(f32)
    return jnp.sum(values, axis=1, keepdims=True).astype(jnp.int32)


def turn_kernel(row_share, col_share, owner_ref, rows_ref, cols_ref, wire_ref, columns_ref, folded_ref, slots):
    held_rows = columns_ref.shape[0]
    fsdp_count = wire_ref.shape[0]
    per_half = per_half_of(row_share)
    pitch = pitch_of(col_share)
    live_rows = owned_extent(owner_ref, rows_ref)
    live_cols = owned_extent(owner_ref, cols_ref) - lax.axis_index("replica") * col_share
    from_wire(slots, wire_ref)
    shape = (held_rows, fsdp_count)
    col_live = (iota(shape, 0) < live_cols) & (iota(shape, 0) < col_share)
    pieces = []
    for h in range(wire_halves):
        turned = get_half(slots, h).T
        for i in range(h * per_half, min(row_share, (h + 1) * per_half)):
            start = (i - h * per_half) * pitch
            keep = col_live & (iota(shape, 1) * row_share + i < live_rows)
            pieces.append(jnp.where(keep, turned[start : start + held_rows], 0.0))
    columns = jnp.concatenate(pieces, axis=1)
    columns_ref[...] = columns.astype(bf16)
    folded_ref[...] = folded(columns, col_share).astype(bf16)


def update_kernel(
    row_share, col_share, owner_ref, rows_ref, cols_ref, block_ref, right_ref, left_high_ref,
    left_low_hbm, wire_hbm, slots, wire_ref, left_low_ref, sem,
):
    copy = pltpu.make_async_copy(left_low_hbm, left_low_ref, sem.at[0])
    copy.start()
    block_order = left_high_ref.shape[0]
    fsdp_count = block_order // row_share
    per_half = per_half_of(row_share)
    pitch = pitch_of(col_share)
    half = right_ref.shape[0] // 8
    live_rows = owned_extent(owner_ref, rows_ref)
    live_cols = owned_extent(owner_ref, cols_ref) - lax.axis_index("replica") * col_share
    whole = block_order // lane_count * lane_count
    rest = jnp.dot(right_ref[2 * half :], block_ref[:, whole:], preferred_element_type=f32)
    rest = rest[:, block_order - whole :].reshape(3, 2, half, block_order // 3)
    total = jnp.dot(
        right_ref[: 2 * half], block_ref[:, :block_order], preferred_element_type=f32
    )
    product = total[:half] + total[half:]
    product += jnp.concatenate([rest[t, 0] + rest[t, 1] for t in range(3)], axis=1)
    product = jnp.concatenate(
        [product, jnp.zeros((lane_count - half, block_order), f32)], axis=0
    )
    high = product.astype(bf16)
    low = (product - high.astype(f32)).astype(bf16)
    last = (((1,), (1,)), ((), ()))
    first = lax.dot_general(
        left_high_ref[...], jnp.concatenate([high, low], axis=0), last, preferred_element_type=f32
    )
    copy.wait()
    count = fsdp_count // send_parts
    shape = (count, lane_count)
    lane = iota(shape, 1)
    col_live = (lane < live_cols) & (lane < col_share)
    sends = []
    for q in range(send_parts):
        held = slice(q * row_share * count, (q + 1) * row_share * count)
        second = lax.dot_general(left_low_ref[held], high, last, preferred_element_type=f32)
        result = first[held, :lane_count] + first[held, lane_count:] + second
        for h in range(wire_halves):
            pieces = []
            for i in range(h * per_half, min(row_share, (h + 1) * per_half)):
                keep = col_live & ((iota(shape, 0) + q * count) * row_share + i < live_rows)
                piece = jnp.where(keep, result[i * count : (i + 1) * count], 0.0)
                pieces.append(piece[:, :pitch])
            value = joined(pieces, wire_ref.shape[2])
            for t, part in enumerate(tiles(value.shape[1])):
                place = pl.ds(q * count * wire_halves + h, count, stride=wire_halves)
                slots[t, place, :] = value[:, part]
        owners = slice(q * count, (q + 1) * count)
        for t, part in enumerate(tiles(wire_ref.shape[2])):
            rows = slots[t, q * count * wire_halves : (q + 1) * count * wire_halves].astype(bf16)
            wire_ref[owners, :, part] = rows.reshape(count, wire_halves, lane_count)
        send = pltpu.make_async_copy(
            wire_ref.at[pl.ds(q * count, count)],
            wire_hbm.at[pl.ds(q * count, count)],
            sem.at[1 + q],
        )
        send.start()
        sends.append(send)
    for send in sends:
        send.wait()


def stats_kernel(row_share, col_share, block_ref, columns_ref, after_ref, left_ref, right_ref):
    held_rows, block_order = columns_ref.shape
    order = order_matrix(row_share, block_order // row_share, True)
    rows_start = lax.axis_index("replica") * col_share
    shape = (block_order, col_share)
    mine = one_hot(iota(shape, 0) == iota(shape, 1) + rows_start)
    replica_count = block_order // col_share
    quarter = col_share // 4
    piece = block_order // 3
    held_rows = block_ref.shape[0] // replica_count
    top = block_ref[:, :block_order]
    rest = block_ref[:, block_order:]
    columns = columns_ref[...]
    last = (((1,), (1,)), ((), ()))
    first = (((0,), (0,)), ((), ()))
    with_top = lax.dot_general(columns, top, last, preferred_element_type=f32)
    natural_rest, with_rest = [], []
    for t in range(3):
        held = slice(t * piece, (t + 1) * piece)
        natural_rest.append(jnp.dot(rest, order[held], preferred_element_type=f32))
        with_rest.append(
            lax.dot_general(columns[:, held], rest, last, preferred_element_type=f32)
        )
    natural = jnp.dot(top, order, preferred_element_type=f32).astype(bf16)
    picked = jnp.dot(natural, mine, preferred_element_type=f32).astype(bf16)
    left = lax.dot_general(picked, natural, first, preferred_element_type=f32)
    for n in range(replica_count):
        held = [n * held_rows + t * quarter for t in range(3)]
        natural = sum(natural_rest[t][held[t] : held[t] + quarter] for t in range(3)).astype(bf16)
        picked = jnp.dot(natural, mine, preferred_element_type=f32).astype(bf16)
        left += lax.dot_general(picked, natural, first, preferred_element_type=f32)
        start = n * col_share
        right_ref[:, start : start + 3 * quarter] = with_top[
            :col_share, n * held_rows : n * held_rows + 3 * quarter
        ]
        right_ref[:, start + 3 * quarter : start + col_share] = sum(
            with_rest[t][:col_share, held[t] : held[t] + quarter] for t in range(3)
        )
    left_ref[...] = left


def body(grad, owner, row_extent, col_extent, left_old, right_old, left_root, right_root):
    fsdp_count = lax.axis_size("fsdp")
    replica_count = lax.axis_size("replica")
    block_count, row_share, col_share = grad.shape
    block_order = row_share * fsdp_count
    lanes = wire_lanes(row_share, col_share)
    wire = pltpu.VMEM((fsdp_count, wire_halves, lanes), bf16)
    slots = pltpu.VMEM((lanes // lane_count, fsdp_count * wire_halves + 8, lane_count), f32)
    owner_row, live_rows, live_cols = owner[None, :], row_extent[None, :], col_extent[None, :]
    turned_grad = grad.transpose(1, 0, 2)

    def exchange(sent):
        return lax.all_to_all(sent, "fsdp", split_axis=0, concat_axis=0, tiled=True)

    received = exchange(
        call(
            pack_kernel,
            wire,
            [hbm, hbm],
            "pack",
            2**20,
            [
                pltpu.VMEM(owner_row.shape, jnp.int32),
                pltpu.VMEM(turned_grad.shape, bf16),
                slots,
                pltpu.SemaphoreType.DMA((2,)),
            ],
        )(pltpu.with_memory_space_constraint(owner_row, pltpu.HBM),
          pltpu.with_memory_space_constraint(turned_grad, pltpu.HBM))
    )

    root_shape = (block_order, block_order)
    half = rounded_up(col_share, 16)
    held_rows = rounded_up(col_share, 8)
    folded_shape = (rounded_up(col_share // 4 * 3, 16), block_order // 3 * 4)
    left_high, left_low, right_pieces = call(
        functools.partial(prepare_kernel, row_share),
        [
            jax.ShapeDtypeStruct(root_shape, bf16),
            pltpu.HBM(root_shape, bf16),
            jax.ShapeDtypeStruct((8 * half, replica_count * folded_shape[0]), bf16),
        ],
        [vmem, vmem],
        "prepare",
        2**31,
        [pltpu.VMEM(root_shape, bf16), pltpu.SemaphoreType.DMA((1,))],
        [vmem, hbm, vmem],
    )(left_root[0], right_root[0])

    columns, sent = call(
        functools.partial(turn_kernel, row_share, col_share),
        [
            jax.ShapeDtypeStruct((held_rows, block_order), bf16),
            jax.ShapeDtypeStruct(folded_shape, bf16),
        ],
        [vmem] * 4,
        "turn",
        2**20,
        [slots],
    )(owner_row, live_rows, live_cols, received)
    block = lax.all_gather(sent, "replica", axis=0, tiled=True)
    result = call(
        functools.partial(update_kernel, row_share, col_share),
        pltpu.HBM(wire.shape, bf16),
        [vmem] * 6 + [hbm],
        "update",
        2**30,
        [slots, wire, pltpu.VMEM(root_shape, bf16), pltpu.SemaphoreType.DMA((1 + send_parts,))],
        hbm,
    )(
        owner_row,
        live_rows,
        live_cols,
        block,
        right_pieces,
        left_high,
        pltpu.with_memory_space_constraint(left_low, pltpu.HBM),
    )
    returned = exchange(result)

    stat = jax.ShapeDtypeStruct((col_share, block_order), f32)
    left_rows, right_rows = call(
        functools.partial(stats_kernel, row_share, col_share),
        [stat, stat],
        [vmem, vmem, hbm],
        "stats",
        2**29,
    )(block, columns, result)
    left_new = decay_rate * left_old + ((1.0 - decay_rate) * left_rows)[None]
    right_new = decay_rate * right_old + ((1.0 - decay_rate) * right_rows)[None]

    update = call(
        unpack_kernel,
        jax.ShapeDtypeStruct((row_share, block_count, col_share), bf16),
        [vmem, vmem],
        "unpack",
        2**20,
        [slots],
    )(owner_row, returned)
    return (update.transpose(1, 0, 2), left_new, right_new)


def solution(mesh):
    placed = (
        P(None, "fsdp", "replica"),
        P(),
        P(),
        P(),
        P("fsdp", "replica", None),
        P("fsdp", "replica", None),
        P("fsdp", None, None),
        P("fsdp", "replica", None),
    )
    return jax.shard_map(
        body,
        mesh=mesh,
        in_specs=placed,
        out_specs=(
            P(None, "fsdp", "replica"),
            P("fsdp", "replica", None),
            P("fsdp", "replica", None),
        ),
        check_vma=False,
    )
```
